32 devices in a mesh: grp: 2 (over x), date: 16 (over z, y, core).
Axes of the slice: x: 2, y: 2, z: 4, core: 2. Of those that a mesh axis runs over, the one named last changes fastest.
Arguments:
- slc: bfloat16 [16, 2, 128, 2048], P('date', None, 'grp'), parts along dimension 2, may hold values from -6 to 6
- pairs: int32 [64, 2], replicated, may hold values from 0 to 15, as said below
- inverse: bfloat16 [15, 64], replicated, may hold values from -6 to 6
Outputs:
- series: float32 [15, 32, 128], P(None, ('grp', 'date')), parts along dimension 1
The draws below stay inside these ranges and needn't reach their ends.
There are 2 independent parts, one for each index of `grp`. The reference program is written for one: setup_inputs(seed, part) draws one part's arguments, and reference() takes and returns one part's arrays. A program takes and returns all parts, laid end to end along the dimension named above; an argument that names none is the same for every part. Nothing has to cross between parts.
Inputs may be any that keep to these rules, and one draw needn't show every extreme that they name: pairs[p,0] < pairs[p,1] for every pair.
All inputs are finite; a program needn't handle non-finite values.
Results may differ from the reference program's by a relative error of at most 0.0003.
Values may be sent and summed in bfloat16 or wider, within the bound.
A program may use at most 128 MiB of HBM per device.

```python
import jax
import jax.numpy as jnp
from jax import lax

COLS = 2048
LOOK_R = 4
LOOK_C = 16
NDATE = 16
STEPS = 15
PAIRS = 64
ROWS = 64


def draw_pairs(key, part):
    key_ref, key_gap = jax.random.split(jax.random.fold_in(key, 11))
    first = jax.random.randint(key_ref, (PAIRS,), 0, NDATE - 1)
    gap = jax.random.randint(key_gap, (PAIRS,), 1, NDATE // 2 + 1)
    second = jnp.minimum(first + gap, NDATE - 1)
    first = first.at[0].set(0)
    second = second.at[PAIRS - 1].set(NDATE - 1)
    return jnp.stack([first, second], axis=1).astype(jnp.int32)


def steps_of(stream_key, dims, cuts, low, top_value):
    loudness = 1.0
    for axis_at, blocks in cuts:
        draws = jax.random.uniform(jax.random.fold_in(jax.random.fold_in(stream_key, 6), axis_at), (blocks,), jnp.float32, low / len(cuts), top_value / len(cuts))
        loudness = loudness * jnp.repeat(jnp.exp(draws), dims[axis_at] // blocks).reshape((-1,) + (1,) * (len(dims) - 1 - axis_at))
    return loudness


def scatter_about(rng, shape, width, reach, shards=(), kind=jnp.bfloat16):
    drawn = width * jax.random.normal(rng, shape, jnp.float32)
    if shards:
        drawn = drawn * steps_of(rng, shape, shards, -0.22, 0.18)
    return jnp.clip(drawn, -reach, reach).astype(kind)


def setup_inputs(seed: int = 0, part: int = 0) -> dict:
    key_of = jax.random.split(jax.random.key(seed), 4)
    part_keys = jax.random.split(jax.random.fold_in(key_of[3], part), 4)
    return {
        "slc": scatter_about(part_keys[0], (NDATE, 2, ROWS, COLS), 1.0, 6.0, ((0, 16),)),
        "pairs": draw_pairs(jax.random.fold_in(key_of[3], 71), part),
        "inverse": scatter_about(key_of[2], (STEPS, PAIRS), (max(PAIRS // 64, 1)) ** -0.5, 6.0),
    }


def boxsum(values):
    count, rows, cols = values.shape
    return values.reshape(count, rows // LOOK_R, LOOK_R, cols // LOOK_C, LOOK_C).sum(axis=(2, 4))

def reference(slc, pairs, inverse):
    first = jnp.take(slc, pairs[:, 0], axis=0).astype(jnp.float32)
    second = jnp.take(slc, pairs[:, 1], axis=0).astype(jnp.float32)
    cross = first[:, 1] * second[:, 0] - first[:, 0] * second[:, 1]
    power_ref = first[:, 0] * first[:, 0] + first[:, 1] * first[:, 1]
    power_sec = second[:, 0] * second[:, 0] + second[:, 1] * second[:, 1]
    looked_cross = boxsum(cross)
    looked_ref = boxsum(power_ref)
    looked_sec = boxsum(power_sec)
    proxy = looked_cross / jnp.sqrt(looked_ref * looked_sec + 1e-06)
    return jnp.einsum('sp,pxy->sxy', inverse.astype(jnp.float32), proxy, precision=lax.Precision.HIGHEST)
```

```python
import functools

import jax
import jax.numpy as jnp
from jax import lax
from jax.experimental import pallas as pl
from jax.experimental.pallas import tpu as pltpu
from jax.sharding import PartitionSpec as P

LOOK_R = 4
LOOK_C = 16
LANES = 128
BLOCK = 16


def split(x):
    high = x.astype(jnp.bfloat16)
    low = (x - high.astype(jnp.float32)).astype(jnp.bfloat16)
    return high, low


def kernel(
    n,
    slc_hbm,
    pairs_hbm,
    inverse_hbm,
    out_ref,
    tile,
    pairs,
    pairs_v,
    inverse,
    stage,
    send,
    recv,
    wide,
    rowsum,
    window,
    in_sem,
    small_sem,
    own_sem,
    send_sem,
    recv_sem,
):
    me = lax.axis_index("date")
    half = n // 2
    rows, cols = tile.shape[1], tile.shape[2]
    chunks = cols // LANES
    blocks = rows // BLOCK
    near = blocks // 2
    per = BLOCK // LOOK_R
    npair = pairs.shape[1]
    base = (me // half) * half
    other = half - base
    block_base = (me // half) * near
    block_other = near - block_base

    def load(k):
        at = pl.ds(pl.multiple_of(block_at(k) * BLOCK, BLOCK), BLOCK)
        return pltpu.make_async_copy(
            slc_hbm.at[0, :, at, :], tile.at[:, at, :], in_sem.at[k]
        )

    def block_at(k):
        if isinstance(k, int):
            first = block_other if k < near else block_base
        else:
            first = jnp.where(k < near, block_other, block_base)
        return first + (me // per + k) % near

    smalls = [
        pltpu.make_async_copy(pairs_hbm, pairs, small_sem.at[0]),
        pltpu.make_async_copy(pairs_hbm, pairs_v, small_sem.at[1]),
        pltpu.make_async_copy(inverse_hbm, inverse, small_sem.at[2]),
    ]
    for k in range(blocks):
        load(k).start()
    for copy in smalls:
        copy.start()

    barrier = pltpu.get_barrier_semaphore()

    def greet(k, _):
        pl.semaphore_signal(
            barrier, inc=1, device_id={"date": (me + k) % n}, device_id_type=pl.DeviceIdType.MESH
        )
        return 0

    lax.fori_loop(1, n, greet, 0)

    def regroup(k):
        block = block_at(k)
        at = pl.ds(pl.multiple_of(block * BLOCK, BLOCK), BLOCK)
        for part in range(2):
            for c in range(chunks):
                piece = tile[part, at, c * LANES : (c + 1) * LANES].astype(jnp.float32)
                stage[part, pl.ds(c, BLOCK, stride=chunks), :] = piece
        for j in range(per):
            for part in range(2):
                span = LOOK_R * chunks
                send[block * per + j, part] = stage[
                    part, j * span : (j + 1) * span, :
                ].astype(jnp.bfloat16)

    def remote(to, came):
        return pltpu.make_async_remote_copy(
            src_ref=send.at[to],
            dst_ref=recv.at[came],
            send_sem=send_sem.at[to],
            recv_sem=recv_sem.at[came],
            device_id={"date": to},
            device_id_type=pl.DeviceIdType.MESH,
        )

    def post(k):
        block = block_at(k)
        for j in range(per):
            to = block * per + (me + j) % per

            @pl.when(to != me)
            def _():
                remote(to, me).start()

    load(0).wait()
    regroup(0)
    pl.semaphore_wait(barrier, n - 1)
    post(0)

    def rest(k, _):
        load(k).wait()
        regroup(k)
        post(k)
        return 0

    lax.fori_loop(1, blocks, rest, 0)

    for copy in smalls:
        copy.wait()

    col = lax.broadcasted_iota(jnp.int32, (cols, cols // LOOK_C), 0) // LOOK_C
    win = lax.broadcasted_iota(jnp.int32, (cols, cols // LOOK_C), 1)
    window[...] = jnp.where(col == win, 1.0, 0.0).astype(jnp.bfloat16)

    def over_rows(x):
        return x.reshape(LOOK_R, chunks, LANES).sum(axis=0)

    def widen(source, block):
        x = block.astype(jnp.float32)
        wide[source] = x
        rowsum[npair + source] = over_rows(x[0] * x[0] + x[1] * x[1])

    widen(me, send[me])

    def arrive(k, _):
        source = jnp.where(k < half, other + (me + k) % half, base + (me + k + 1) % half)
        remote(source, source).wait_recv()
        widen(source, recv[source])
        return 0

    lax.fori_loop(0, n - 1, arrive, 0)

    def pair(p, _):
        a = pairs[0, p]
        b = pairs[1, p]
        cross = wide[a, 1] * wide[b, 0] - wide[a, 0] * wide[b, 1]
        rowsum[p] = over_rows(cross)
        return 0

    lax.fori_loop(0, npair, pair, 0, unroll=4)

    total = npair + n
    looked = jnp.zeros((total, cols // LOOK_C), jnp.float32)
    for c in range(chunks):
        high, low = split(rowsum[:, c, :])
        weight = window[c * LANES : (c + 1) * LANES, :]
        looked += jnp.dot(high, weight, preferred_element_type=jnp.float32)
        looked += jnp.dot(low, weight, preferred_element_type=jnp.float32)
    powers = looked[npair:]
    date = lax.broadcasted_iota(jnp.int32, (n, npair), 0)

    def pick(which):
        hot = jnp.where(pairs_v[which : which + 1, :] == date, 1.0, 0.0)
        return lax.dot_general(
            hot,
            powers,
            (((0,), (0,)), ((), ())),
            precision=lax.Precision.HIGHEST,
            preferred_element_type=jnp.float32,
        )

    proxy = looked[:npair] / jnp.sqrt(pick(0) * pick(1) + 1e-06)
    high, low = split(proxy)
    series = jnp.dot(inverse[...], high, preferred_element_type=jnp.float32)
    series += jnp.dot(inverse[...], low, preferred_element_type=jnp.float32)
    out_ref[...] = series.reshape(out_ref.shape)

    def left(k, _):
        remote((me + k) % n, me).wait_send()
        return 0

    lax.fori_loop(1, n, left, 0)


def per_device(n, slc, pairs, inverse):
    _, _, rows, cols = slc.shape
    steps, npair = inverse.shape
    chunks = cols // LANES
    span = LOOK_R * chunks
    pairs = pairs.T
    return pl.pallas_call(
        functools.partial(kernel, n),
        out_shape=jax.ShapeDtypeStruct((steps, 1, cols // LOOK_C), jnp.float32),
        in_specs=[pl.BlockSpec(memory_space=pltpu.HBM)] * 3,
        out_specs=pl.BlockSpec(memory_space=pltpu.VMEM),
        scratch_shapes=[
            pltpu.VMEM((2, rows, cols), jnp.bfloat16),
            pltpu.SMEM((2, npair), jnp.int32),
            pltpu.VMEM((2, npair), jnp.int32),
            pltpu.VMEM((steps, npair), jnp.bfloat16),
            pltpu.VMEM((2, BLOCK * chunks, LANES), jnp.float32),
            pltpu.VMEM((n, 2, span, LANES), jnp.bfloat16),
            pltpu.VMEM((n, 2, span, LANES), jnp.bfloat16),
            pltpu.VMEM((n, 2, span, LANES), jnp.float32),
            pltpu.VMEM((npair + n, chunks, LANES), jnp.float32),
            pltpu.VMEM((cols, cols // LOOK_C), jnp.bfloat16),
            pltpu.SemaphoreType.DMA((rows // BLOCK,)),
            pltpu.SemaphoreType.DMA((3,)),
            pltpu.SemaphoreType.DMA,
            pltpu.SemaphoreType.DMA((n,)),
            pltpu.SemaphoreType.DMA((n,)),
        ],
        compiler_params=pltpu.CompilerParams(
            collective_id=0, has_side_effects=True, vmem_limit_bytes=48 * 1024 * 1024
        ),
    )(slc, pairs, inverse)


def solution(mesh):
    n = mesh.shape["date"]
    in_specs = (P("date", None, "grp", None), P(), P())
    out_specs = P(None, ("grp", "date"), None)
    return jax.shard_map(
        functools.partial(per_device, n),
        mesh=mesh,
        in_specs=in_specs,
        out_specs=out_specs,
        check_vma=False,
    )
```

```python
import functools

import jax
import jax.numpy as jnp
from jax import lax
from jax.experimental import pallas as pl
from jax.experimental.pallas import tpu as pltpu
from jax.sharding import PartitionSpec as P

LOOK_R = 4
LOOK_C = 16
LANES = 128
BLOCK = 16
PIECES = 2


def split(x):
    high = x.astype(jnp.bfloat16)
    low = (x - high.astype(jnp.float32)).astype(jnp.bfloat16)
    return high, low


def kernel(
    n,
    pieces,
    slc_hbm,
    pairs_hbm,
    inverse_hbm,
    out_ref,
    tile,
    pairs,
    pairs_v,
    inverse,
    stage,
    send,
    recv,
    wide,
    rowsum,
    window,
    hot,
    in_sem,
    small_sem,
    send_sem,
    recv_sem,
):
    me = lax.axis_index("date")
    half = n // 2
    rows, cols = tile.shape[1], tile.shape[2]
    chunks = cols // LANES // pieces
    span = LOOK_R * chunks
    blocks = rows // BLOCK
    near = blocks // 2
    per = BLOCK // LOOK_R
    npair = pairs.shape[1]
    total = npair + n
    group = rowsum.shape[0] // total
    base = (me // half) * half
    other = half - base
    block_base = (me // half) * near
    block_other = near - block_base

    def block_at(k):
        if isinstance(k, int):
            first = block_other if k < near else block_base
        else:
            first = jnp.where(k < near, block_other, block_base)
        return first + (me // per + k) % near

    def load(k):
        at = pl.ds(pl.multiple_of(block_at(k) * BLOCK, BLOCK), BLOCK)
        return pltpu.make_async_copy(
            slc_hbm.at[0, :, at, :], tile.at[:, at, :], in_sem.at[k]
        )

    smalls = [
        pltpu.make_async_copy(pairs_hbm, pairs, small_sem.at[0]),
        pltpu.make_async_copy(pairs_hbm, pairs_v, small_sem.at[1]),
        pltpu.make_async_copy(inverse_hbm, inverse, small_sem.at[2]),
    ]
    barrier = pltpu.get_barrier_semaphore()

    def greet(k, _):
        pl.semaphore_signal(
            barrier, inc=1, device_id={"date": (me + k) % n}, device_id_type=pl.DeviceIdType.MESH
        )
        return 0

    for k in range(blocks):
        load(k).start()
    lax.fori_loop(1, n, greet, 0)
    for copy in smalls:
        copy.start()

    def regroup(k):
        block = block_at(k)
        at = pl.ds(pl.multiple_of(block * BLOCK, BLOCK), BLOCK)
        for q in range(pieces):
            for part in range(2):
                for c in range(chunks):
                    column = (q * chunks + c) * LANES
                    piece = tile[part, at, column : column + LANES].astype(jnp.float32)
                    stage[q, part, pl.ds(c, BLOCK, stride=chunks), :] = piece
            for j in range(per):
                send[q, block * per + j] = stage[
                    q, :, j * span : (j + 1) * span, :
                ].astype(jnp.bfloat16)

    def remote(q, to, came):
        return pltpu.make_async_remote_copy(
            src_ref=send.at[q, to],
            dst_ref=recv.at[q, came],
            send_sem=send_sem.at[q, to],
            recv_sem=recv_sem.at[q, came],
            device_id={"date": to},
            device_id_type=pl.DeviceIdType.MESH,
        )

    def post(q, k):
        block = block_at(k)
        for j in range(per):
            to = block * per + (me + j) % per

            @pl.when(to != me)
            def _():
                remote(q, to, me).start()

    load(0).wait()
    regroup(0)
    pl.semaphore_wait(barrier, n - 1)
    post(0, 0)

    def rest(k, _):
        load(k).wait()
        regroup(k)
        post(0, k)
        return 0

    lax.fori_loop(1, blocks, rest, 0)

    for q in range(1, pieces):

        def more(k, _):
            post(q, k)
            return 0

        lax.fori_loop(0, blocks, more, 0)

    for copy in smalls:
        copy.wait()

    col = lax.broadcasted_iota(jnp.int32, window.shape, 0) // LOOK_C
    win = lax.broadcasted_iota(jnp.int32, window.shape, 1)
    window[...] = jnp.where(col == win, 1.0, 0.0).astype(jnp.bfloat16)
    date = lax.broadcasted_iota(jnp.int32, (n, npair), 0)
    for which in range(2):
        flag = jnp.where(pairs_v[which : which + 1, :] == date, 1.0, 0.0)
        hot[which * npair : (which + 1) * npair, :] = flag.T.astype(jnp.bfloat16)

    def over_rows(x):
        return x.reshape(-1, group, LANES).sum(axis=0)

    def keep(row, x):
        rowsum[pl.ds(pl.multiple_of(row * group, group), group), :] = over_rows(x)

    looked = jnp.zeros((total, window.shape[1]), jnp.float32)
    for q in range(pieces):

        def widen(source, block):
            x = block.astype(jnp.float32)
            wide[source] = x
            keep(npair + source, x[0] * x[0] + x[1] * x[1])

        def arrive(k, _):
            source = jnp.where(
                k < half, other + (me + k) % half, base + (me + k + 1) % half
            )
            remote(q, source, source).wait_recv()
            widen(source, recv[q, source])
            return 0

        def pair(p, _):
            a = pairs[0, p]
            b = pairs[1, p]
            keep(p, wide[a, 1] * wide[b, 0] - wide[a, 0] * wide[b, 1])
            return 0

        widen(me, send[q, me])
        lax.fori_loop(0, n - 1, arrive, 0)
        lax.fori_loop(0, npair, pair, 0, unroll=8)

        columns = []
        for c in range(chunks):
            x = rowsum[pl.ds(c, total, stride=group), :]
            for again in range(c + chunks, group, chunks):
                x += rowsum[pl.ds(again, total, stride=group), :]
            columns.append(x)
        high, low = split(jnp.concatenate(columns, axis=1))
        depth = chunks * LANES
        sums = jnp.dot(
            jnp.concatenate([high, low], axis=0),
            window[q * depth : (q + 1) * depth, :],
            preferred_element_type=jnp.float32,
        )
        looked += sums[:total] + sums[total:]

    def exact(left, x):
        width = x.shape[1]
        both = jnp.concatenate(split(x), axis=1)
        y = jnp.dot(left, both, preferred_element_type=jnp.float32)
        return y[:, :width] + y[:, width:]

    powers = exact(hot[...], looked[npair:])
    proxy = looked[:npair] / jnp.sqrt(powers[:npair] * powers[npair:] + 1e-06)
    out_ref[...] = exact(inverse[...], proxy).reshape(out_ref.shape)

    def left(k, _):
        for q in range(pieces):
            remote(q, (me + k) % n, me).wait_send()
        return 0

    lax.fori_loop(1, n, left, 0)


def per_device(n, slc, pairs, inverse):
    _, _, rows, cols = slc.shape
    steps, npair = inverse.shape
    pieces = PIECES
    chunks = cols // LANES // pieces
    span = LOOK_R * chunks
    group = max(chunks, 8)
    windows = cols // LOOK_C
    return pl.pallas_call(
        functools.partial(kernel, n, pieces),
        out_shape=jax.ShapeDtypeStruct((steps, 1, windows), jnp.float32),
        in_specs=[pl.BlockSpec(memory_space=pltpu.HBM)] * 3,
        out_specs=pl.BlockSpec(memory_space=pltpu.VMEM),
        scratch_shapes=[
            pltpu.VMEM((2, rows, cols), jnp.bfloat16),
            pltpu.SMEM((2, npair), jnp.int32),
            pltpu.VMEM((2, npair), jnp.int32),
            pltpu.VMEM((steps, npair), jnp.bfloat16),
            pltpu.VMEM((pieces, 2, BLOCK * chunks, LANES), jnp.float32),
            pltpu.VMEM((pieces, n, 2, span, LANES), jnp.bfloat16),
            pltpu.VMEM((pieces, n, 2, span, LANES), jnp.bfloat16),
            pltpu.VMEM((n, 2, span, LANES), jnp.float32),
            pltpu.VMEM(((npair + n) * group, LANES), jnp.float32),
            pltpu.VMEM((cols, windows), jnp.bfloat16),
            pltpu.VMEM((2 * npair, n), jnp.bfloat16),
            pltpu.SemaphoreType.DMA((rows // BLOCK,)),
            pltpu.SemaphoreType.DMA((3,)),
            pltpu.SemaphoreType.DMA((pieces, n)),
            pltpu.SemaphoreType.DMA((pieces, n)),
        ],
        compiler_params=pltpu.CompilerParams(
            collective_id=0, has_side_effects=True, vmem_limit_bytes=63 * 1024 * 1024
        ),
    )(slc, pairs.T, inverse)


def solution(mesh):
    n = mesh.shape["date"]
    in_specs = (P("date", None, "grp", None), P(), P())
    out_specs = P(None, ("grp", "date"), None)
    return jax.shard_map(
        functools.partial(per_device, n),
        mesh=mesh,
        in_specs=in_specs,
        out_specs=out_specs,
        check_vma=False,
    )
```

```python
import functools

import jax
import jax.numpy as jnp
from jax import lax
from jax.experimental import pallas as pl
from jax.experimental.pallas import tpu as pltpu
from jax.sharding import PartitionSpec as P

LOOK_R = 4
LOOK_C = 16
LANES = 128
BLOCK = 16
PIECES = 2


def split(x):
    high = x.astype(jnp.bfloat16)
    low = (x - high.astype(jnp.float32)).astype(jnp.bfloat16)
    return high, low


def kernel(
    n,
    pieces,
    slc_hbm,
    pairs_hbm,
    inverse_hbm,
    out_ref,
    tile,
    pairs,
    pairs_v,
    inverse,
    stage,
    send,
    recv,
    wide,
    rowsum,
    window,
    hot,
    in_sem,
    small_sem,
    send_sem,
    recv_sem,
):
    me = lax.axis_index("date")
    half = n // 2
    rows, cols = tile.shape[1], tile.shape[2]
    chunks = cols // LANES // pieces
    span = LOOK_R * chunks
    blocks = rows // BLOCK
    near = blocks // 2
    per = BLOCK // LOOK_R
    npair = pairs.shape[1]
    total = npair + n
    group = rowsum.shape[0] // total
    base = (me // half) * half
    other = half - base
    block_base = (me // half) * near
    block_other = near - block_base

    phase = (me // per) % 2

    def block_at(k):
        first = jnp.where((k + phase) % 2 == 0, block_other, block_base)
        return first + (me // per + k // 2) % near

    def load(k):
        at = pl.ds(pl.multiple_of(block_at(k) * BLOCK, BLOCK), BLOCK)
        return pltpu.make_async_copy(
            slc_hbm.at[0, :, at, :], tile.at[:, at, :], in_sem.at[k]
        )

    smalls = [
        pltpu.make_async_copy(pairs_hbm, pairs, small_sem.at[0]),
        pltpu.make_async_copy(pairs_hbm, pairs_v, small_sem.at[1]),
        pltpu.make_async_copy(inverse_hbm, inverse, small_sem.at[2]),
    ]
    barrier = pltpu.get_barrier_semaphore()

    def greet(k, _):
        pl.semaphore_signal(
            barrier, inc=1, device_id={"date": (me + k) % n}, device_id_type=pl.DeviceIdType.MESH
        )
        return 0

    for k in range(blocks):
        load(k).start()
    lax.fori_loop(1, n, greet, 0)
    for copy in smalls:
        copy.start()

    def regroup(k):
        block = block_at(k)
        at = pl.ds(pl.multiple_of(block * BLOCK, BLOCK), BLOCK)
        for q in range(pieces):
            for part in range(2):
                for c in range(chunks):
                    column = (q * chunks + c) * LANES
                    piece = tile[part, at, column : column + LANES].astype(jnp.float32)
                    stage[q, part, pl.ds(c, BLOCK, stride=chunks), :] = piece
            for j in range(per):
                send[q, block * per + j] = stage[
                    q, :, j * span : (j + 1) * span, :
                ].astype(jnp.bfloat16)

    def remote(q, to, came):
        return pltpu.make_async_remote_copy(
            src_ref=send.at[q, to],
            dst_ref=recv.at[q, came],
            send_sem=send_sem.at[q, to],
            recv_sem=recv_sem.at[q, came],
            device_id={"date": to},
            device_id_type=pl.DeviceIdType.MESH,
        )

    def post(q, k):
        block = block_at(k)
        for j in range(per):
            to = block * per + (me + j) % per

            @pl.when(to != me)
            def _():
                remote(q, to, me).start()

    load(0).wait()
    regroup(0)
    pl.semaphore_wait(barrier, n - 1)
    post(0, 0)

    def rest(k, _):
        load(k).wait()
        regroup(k)
        post(0, k)
        return 0

    lax.fori_loop(1, blocks, rest, 0)

    for q in range(1, pieces):

        def more(k, _):
            post(q, k)
            return 0

        lax.fori_loop(0, blocks, more, 0)

    for copy in smalls:
        copy.wait()

    col = lax.broadcasted_iota(jnp.int32, window.shape, 0) // LOOK_C
    win = lax.broadcasted_iota(jnp.int32, window.shape, 1)
    window[...] = jnp.where(col == win, 1.0, 0.0).astype(jnp.bfloat16)
    date = lax.broadcasted_iota(jnp.int32, (n, npair), 0)
    for which in range(2):
        flag = jnp.where(pairs_v[which : which + 1, :] == date, 1.0, 0.0)
        hot[which * npair : (which + 1) * npair, :] = flag.T.astype(jnp.bfloat16)

    def over_rows(x):
        return x.reshape(-1, group, LANES).sum(axis=0)

    def keep(row, x):
        rowsum[pl.ds(pl.multiple_of(row * group, group), group), :] = over_rows(x)

    looked = jnp.zeros((total, window.shape[1]), jnp.float32)
    for q in range(pieces):

        def widen(source, block):
            x = block.astype(jnp.float32)
            wide[source] = x
            keep(npair + source, x[0] * x[0] + x[1] * x[1])

        def arrive(k, _):
            source = jnp.where(
                k < half, other + (me + k) % half, base + (me + k + 1) % half
            )
            remote(q, source, source).wait_recv()
            widen(source, recv[q, source])
            return 0

        def pair(p, _):
            a = pairs[0, p]
            b = pairs[1, p]
            keep(p, wide[a, 1] * wide[b, 0] - wide[a, 0] * wide[b, 1])
            return 0

        widen(me, send[q, me])
        lax.fori_loop(0, n - 1, arrive, 0)
        lax.fori_loop(0, npair, pair, 0, unroll=8)

        columns = []
        for c in range(chunks):
            x = rowsum[pl.ds(c, total, stride=group), :]
            for again in range(c + chunks, group, chunks):
                x += rowsum[pl.ds(again, total, stride=group), :]
            columns.append(x)
        high, low = split(jnp.concatenate(columns, axis=1))
        depth = chunks * LANES
        sums = jnp.dot(
            jnp.concatenate([high, low], axis=0),
            window[q * depth : (q + 1) * depth, :],
            preferred_element_type=jnp.float32,
        )
        looked += sums[:total] + sums[total:]

    def exact(left, x):
        width = x.shape[1]
        both = jnp.concatenate(split(x), axis=1)
        y = jnp.dot(left, both, preferred_element_type=jnp.float32)
        return y[:, :width] + y[:, width:]

    powers = exact(hot[...], looked[npair:])
    proxy = looked[:npair] / jnp.sqrt(powers[:npair] * powers[npair:] + 1e-06)
    out_ref[...] = exact(inverse[...], proxy).reshape(out_ref.shape)

    def left(k, _):
        for q in range(pieces):
            remote(q, (me + k) % n, me).wait_send()
        return 0

    lax.fori_loop(1, n, left, 0)


def per_device(n, slc, pairs, inverse):
    _, _, rows, cols = slc.shape
    steps, npair = inverse.shape
    pieces = PIECES
    chunks = cols // LANES // pieces
    span = LOOK_R * chunks
    group = max(chunks, 8)
    windows = cols // LOOK_C
    return pl.pallas_call(
        functools.partial(kernel, n, pieces),
        out_shape=pltpu.VMEM((steps, 1, windows), jnp.float32),
        in_specs=[pl.BlockSpec(memory_space=pltpu.HBM)] * 3,
        out_specs=pl.BlockSpec(memory_space=pltpu.VMEM),
        scratch_shapes=[
            pltpu.VMEM((2, rows, cols), jnp.bfloat16),
            pltpu.SMEM((2, npair), jnp.int32),
            pltpu.VMEM((2, npair), jnp.int32),
            pltpu.VMEM((steps, npair), jnp.bfloat16),
            pltpu.VMEM((pieces, 2, BLOCK * chunks, LANES), jnp.float32),
            pltpu.VMEM((pieces, n, 2, span, LANES), jnp.bfloat16),
            pltpu.VMEM((pieces, n, 2, span, LANES), jnp.bfloat16),
            pltpu.VMEM((n, 2, span, LANES), jnp.float32),
            pltpu.VMEM(((npair + n) * group, LANES), jnp.float32),
            pltpu.VMEM((cols, windows), jnp.bfloat16),
            pltpu.VMEM((2 * npair, n), jnp.bfloat16),
            pltpu.SemaphoreType.DMA((rows // BLOCK,)),
            pltpu.SemaphoreType.DMA((3,)),
            pltpu.SemaphoreType.DMA((pieces, n)),
            pltpu.SemaphoreType.DMA((pieces, n)),
        ],
        compiler_params=pltpu.CompilerParams(
            collective_id=0, has_side_effects=True, vmem_limit_bytes=63 * 1024 * 1024
        ),
    )(slc, pairs.T, inverse)


def solution(mesh):
    n = mesh.shape["date"]
    in_specs = (P("date", None, "grp", None), P(), P())
    out_specs = P(None, ("grp", "date"), None)
    return jax.shard_map(
        functools.partial(per_device, n),
        mesh=mesh,
        in_specs=in_specs,
        out_specs=out_specs,
        check_vma=False,
    )
```

```python
import functools

import jax
import jax.numpy as jnp
from jax import lax
from jax.experimental import pallas as pl
from jax.experimental.pallas import tpu as pltpu
from jax.sharding import PartitionSpec as P

LOOK_R = 4
LOOK_C = 16
LANES = 128
BLOCK = 16
PIECES = 2


def split(x):
    high = x.astype(jnp.bfloat16)
    low = (x - high.astype(jnp.float32)).astype(jnp.bfloat16)
    return high, low


def kernel(
    n,
    pieces,
    slc_hbm,
    pairs_hbm,
    inverse_hbm,
    out_ref,
    tile,
    pairs,
    pairs_v,
    inverse,
    stage,
    send,
    recv,
    held,
    rowsum,
    window,
    hot,
    in_sem,
    small_sem,
    send_sem,
    recv_sem,
):
    me = lax.axis_index("date")
    half = n // 2
    rows, cols = tile.shape[1], tile.shape[2]
    chunks = cols // LANES // pieces
    span = LOOK_R * chunks
    blocks = rows // BLOCK
    near = blocks // 2
    per = BLOCK // LOOK_R
    npair = pairs.shape[1]
    total = npair + n
    group = rowsum.shape[0] // total
    base = (me // half) * half
    other = half - base
    block_base = (me // half) * near
    block_other = near - block_base

    phase = (me // per) % 2

    def block_at(k):
        first = jnp.where((k + phase) % 2 == 0, block_other, block_base)
        return first + (me // per + k // 2) % near

    def load(k):
        at = pl.ds(pl.multiple_of(block_at(k) * BLOCK, BLOCK), BLOCK)
        return pltpu.make_async_copy(
            slc_hbm.at[0, :, at, :], tile.at[:, at, :], in_sem.at[k]
        )

    smalls = [
        pltpu.make_async_copy(pairs_hbm, pairs, small_sem.at[0]),
        pltpu.make_async_copy(pairs_hbm, pairs_v, small_sem.at[1]),
        pltpu.make_async_copy(inverse_hbm, inverse, small_sem.at[2]),
    ]
    barrier = pltpu.get_barrier_semaphore()

    def greet(k, _):
        pl.semaphore_signal(
            barrier, inc=1, device_id={"date": (me + k) % n}, device_id_type=pl.DeviceIdType.MESH
        )
        return 0

    for k in range(blocks):
        load(k).start()
    lax.fori_loop(1, n, greet, 0)
    for copy in smalls:
        copy.start()

    def regroup(k):
        block = block_at(k)
        at = pl.ds(pl.multiple_of(block * BLOCK, BLOCK), BLOCK)
        for q in range(pieces):
            for part in range(2):
                for c in range(chunks):
                    column = (q * chunks + c) * LANES
                    piece = tile[part, at, column : column + LANES].astype(jnp.float32)
                    stage[q, part, pl.ds(c, BLOCK, stride=chunks), :] = piece
            for j in range(per):
                send[q, block * per + j] = stage[
                    q, :, j * span : (j + 1) * span, :
                ].astype(jnp.bfloat16)

    def remote(q, to, came):
        return pltpu.make_async_remote_copy(
            src_ref=send.at[q, to],
            dst_ref=recv.at[q, came],
            send_sem=send_sem.at[q, to],
            recv_sem=recv_sem.at[q, came],
            device_id={"date": to},
            device_id_type=pl.DeviceIdType.MESH,
        )

    def post(q, k):
        block = block_at(k)
        for j in range(per):
            to = block * per + (me + j) % per

            @pl.when(to != me)
            def _():
                remote(q, to, me).start()

    def fill(k, _):
        load(k).wait()
        regroup(k)

        @pl.when(k == 0)
        def _():
            pl.semaphore_wait(barrier, n - 1)

        post(0, k)
        return 0

    lax.fori_loop(0, blocks, fill, 0)

    def more(k, _):
        post(1 + k // blocks, k % blocks)
        return 0

    lax.fori_loop(0, (pieces - 1) * blocks, more, 0)

    for copy in smalls:
        copy.wait()

    def tile_of_window(c, _):
        shape = (LANES, window.shape[1])
        col = c * (LANES // LOOK_C) + lax.broadcasted_iota(jnp.int32, shape, 0) // LOOK_C
        win = lax.broadcasted_iota(jnp.int32, shape, 1)
        at = pl.ds(pl.multiple_of(c * LANES, LANES), LANES)
        window[at, :] = jnp.where(col == win, 1.0, 0.0).astype(jnp.bfloat16)
        return 0

    lax.fori_loop(0, cols // LANES, tile_of_window, 0)
    date = lax.broadcasted_iota(jnp.int32, (n, npair), 0)
    for which in range(2):
        flag = jnp.where(pairs_v[which : which + 1, :] == date, 1.0, 0.0)
        hot[which * npair : (which + 1) * npair, :] = flag.T.astype(jnp.bfloat16)
    for q in range(pieces):
        recv[q, me] = send[q, me]

    def keep(row, x):
        at = pl.ds(pl.multiple_of(row * group, group), group)
        rowsum[at, :] = x.reshape(-1, group, LANES).sum(axis=0)

    def piece_of(q, looked):
        def arrive(k, _):
            source = jnp.where(
                k < half, other + (me + k) % half, base + (me + k + 1) % half
            )
            remote(q, source, source).wait_recv()
            return 0

        def power(t, _):
            held[t] = recv[q, t]
            x = recv[q, t].astype(jnp.float32)
            keep(npair + t, x[0] * x[0] + x[1] * x[1])
            return 0

        def pair(p, _):
            a = held[pairs[0, p]].astype(jnp.float32)
            b = held[pairs[1, p]].astype(jnp.float32)
            keep(p, a[1] * b[0] - a[0] * b[1])
            return 0

        lax.fori_loop(0, n - 1, arrive, 0)
        lax.fori_loop(0, n, power, 0, unroll=8)
        lax.fori_loop(0, npair, pair, 0, unroll=8)

        columns = []
        for c in range(chunks):
            x = rowsum[pl.ds(c, total, stride=group), :]
            for again in range(c + chunks, group, chunks):
                x += rowsum[pl.ds(again, total, stride=group), :]
            columns.append(x)
        high, low = split(jnp.concatenate(columns, axis=1))
        depth = chunks * LANES
        sums = jnp.dot(
            jnp.concatenate([high, low], axis=0),
            window[pl.ds(pl.multiple_of(q * depth, depth), depth), :],
            preferred_element_type=jnp.float32,
        )
        return looked + sums[:total] + sums[total:]

    looked = jnp.zeros((total, window.shape[1]), jnp.float32)
    looked = lax.fori_loop(0, pieces, piece_of, looked)

    def exact(left, x):
        width = x.shape[1]
        both = jnp.concatenate(split(x), axis=1)
        y = jnp.dot(left, both, preferred_element_type=jnp.float32)
        return y[:, :width] + y[:, width:]

    powers = exact(hot[...], looked[npair:])
    proxy = looked[:npair] * lax.rsqrt(powers[:npair] * powers[npair:] + 1e-06)
    out_ref[...] = exact(inverse[...], proxy).reshape(out_ref.shape)

    def left(k, _):
        for q in range(pieces):
            remote(q, (me + k) % n, me).wait_send()
        return 0

    lax.fori_loop(1, n, left, 0)


def per_device(n, slc, pairs, inverse):
    _, _, rows, cols = slc.shape
    steps, npair = inverse.shape
    pieces = PIECES
    chunks = cols // LANES // pieces
    span = LOOK_R * chunks
    group = max(chunks, 8)
    windows = cols // LOOK_C
    return pl.pallas_call(
        functools.partial(kernel, n, pieces),
        out_shape=pltpu.VMEM((steps, 1, windows), jnp.float32),
        in_specs=[pl.BlockSpec(memory_space=pltpu.HBM)] * 3,
        out_specs=pl.BlockSpec(memory_space=pltpu.VMEM),
        scratch_shapes=[
            pltpu.VMEM((2, rows, cols), jnp.bfloat16),
            pltpu.SMEM((2, npair), jnp.int32),
            pltpu.VMEM((2, npair), jnp.int32),
            pltpu.VMEM((steps, npair), jnp.bfloat16),
            pltpu.VMEM((pieces, 2, BLOCK * chunks, LANES), jnp.float32),
            pltpu.VMEM((pieces, n, 2, span, LANES), jnp.bfloat16),
            pltpu.VMEM((pieces, n, 2, span, LANES), jnp.bfloat16),
            pltpu.VMEM((n, 2, span, LANES), jnp.bfloat16),
            pltpu.VMEM(((npair + n) * group, LANES), jnp.float32),
            pltpu.VMEM((cols, windows), jnp.bfloat16),
            pltpu.VMEM((2 * npair, n), jnp.bfloat16),
            pltpu.SemaphoreType.DMA((rows // BLOCK,)),
            pltpu.SemaphoreType.DMA((3,)),
            pltpu.SemaphoreType.DMA((pieces, n)),
            pltpu.SemaphoreType.DMA((pieces, n)),
        ],
        compiler_params=pltpu.CompilerParams(
            collective_id=0, has_side_effects=True, vmem_limit_bytes=63 * 1024 * 1024
        ),
    )(slc, pairs.T, inverse)


def solution(mesh):
    n = mesh.shape["date"]
    in_specs = (P("date", None, "grp", None), P(), P())
    out_specs = P(None, ("grp", "date"), None)
    return jax.shard_map(
        functools.partial(per_device, n),
        mesh=mesh,
        in_specs=in_specs,
        out_specs=out_specs,
        check_vma=False,
    )
```

```python
import functools

import jax
import jax.numpy as jnp
from jax import lax
from jax.experimental import pallas as pl
from jax.experimental.pallas import tpu as pltpu
from jax.sharding import PartitionSpec as P

LOOK_R = 4
LOOK_C = 16
LANES = 128
BLOCK = 16
PIECES = 2


def split(x):
    high = x.astype(jnp.bfloat16)
    low = (x - high.astype(jnp.float32)).astype(jnp.bfloat16)
    return high, low


def kernel(
    n,
    pieces,
    slc_hbm,
    pairs_hbm,
    inverse_hbm,
    out_ref,
    tile,
    pairs,
    pairs_v,
    inverse,
    stage,
    send,
    recv,
    held,
    rowsum,
    window,
    hot,
    in_sem,
    small_sem,
    send_sem,
    recv_sem,
):
    me = lax.axis_index("date")
    half = n // 2
    rows, cols = tile.shape[1], tile.shape[2]
    chunks = cols // LANES // pieces
    span = LOOK_R * chunks
    blocks = rows // BLOCK
    near = blocks // 2
    per = BLOCK // LOOK_R
    npair = pairs.shape[1]
    total = npair + n
    group = rowsum.shape[0] // total
    base = (me // half) * half
    other = half - base
    block_other = near - (me // half) * near

    def block_at(k):
        return (block_other + k) % blocks

    def load(k):
        at = pl.ds(pl.multiple_of(block_at(k) * BLOCK, BLOCK), BLOCK)
        return pltpu.make_async_copy(
            slc_hbm.at[0, :, at, :], tile.at[:, at, :], in_sem.at[k]
        )

    smalls = [
        pltpu.make_async_copy(pairs_hbm, pairs, small_sem.at[0]),
        pltpu.make_async_copy(pairs_hbm, pairs_v, small_sem.at[1]),
        pltpu.make_async_copy(inverse_hbm, inverse, small_sem.at[2]),
    ]
    barrier = pltpu.get_barrier_semaphore()

    def greet(k, _):
        pl.semaphore_signal(
            barrier, inc=1, device_id={"date": (me + k) % n}, device_id_type=pl.DeviceIdType.MESH
        )
        return 0

    for k in range(blocks):
        load(k).start()
    lax.fori_loop(1, n, greet, 0)
    for copy in smalls:
        copy.start()

    def regroup(k):
        block = block_at(k)
        at = pl.ds(pl.multiple_of(block * BLOCK, BLOCK), BLOCK)
        for q in range(pieces):
            for part in range(2):
                for c in range(chunks):
                    column = (q * chunks + c) * LANES
                    piece = tile[part, at, column : column + LANES].astype(jnp.float32)
                    stage[q, part, pl.ds(c, BLOCK, stride=chunks), :] = piece
            for j in range(per):
                send[q, block * per + j] = stage[
                    q, :, j * span : (j + 1) * span, :
                ].astype(jnp.bfloat16)

    def remote(q, to, came):
        return pltpu.make_async_remote_copy(
            src_ref=send.at[q, to],
            dst_ref=recv.at[q, came],
            send_sem=send_sem.at[q, to],
            recv_sem=recv_sem.at[q, came],
            device_id={"date": to},
            device_id_type=pl.DeviceIdType.MESH,
        )

    def fill(k, _):
        load(k).wait()
        regroup(k)
        return 0

    lax.fori_loop(0, blocks, fill, 0)
    pl.semaphore_wait(barrier, n - 1)

    def post(step, _):
        q = step // half
        at = (me + step) % half
        remote(q, other + at, me).start()

        @pl.when(base + at != me)
        def _():
            remote(q, base + at, me).start()

        return 0

    lax.fori_loop(0, pieces * half, post, 0)

    for copy in smalls:
        copy.wait()

    def tile_of_window(c, _):
        shape = (LANES, window.shape[1])
        col = c * (LANES // LOOK_C) + lax.broadcasted_iota(jnp.int32, shape, 0) // LOOK_C
        win = lax.broadcasted_iota(jnp.int32, shape, 1)
        at = pl.ds(pl.multiple_of(c * LANES, LANES), LANES)
        window[at, :] = jnp.where(col == win, 1.0, 0.0).astype(jnp.bfloat16)
        return 0

    lax.fori_loop(0, cols // LANES, tile_of_window, 0)
    date = lax.broadcasted_iota(jnp.int32, (n, npair), 0)
    for which in range(2):
        flag = jnp.where(pairs_v[which : which + 1, :] == date, 1.0, 0.0)
        hot[which * npair : (which + 1) * npair, :] = flag.T.astype(jnp.bfloat16)
    for q in range(pieces):
        recv[q, me] = send[q, me]

    def keep(row, x):
        at = pl.ds(pl.multiple_of(row * group, group), group)
        rowsum[at, :] = x.reshape(-1, group, LANES).sum(axis=0)

    def piece_of(q, looked):
        def arrive(k, _):
            source = jnp.where(
                k < half, other + (me + k) % half, base + (me + k + 1) % half
            )
            remote(q, source, source).wait_recv()
            return 0

        def power(t, _):
            held[t] = recv[q, t]
            x = recv[q, t].astype(jnp.float32)
            keep(npair + t, x[0] * x[0] + x[1] * x[1])
            return 0

        def pair(p, _):
            a = held[pairs[0, p]].astype(jnp.float32)
            b = held[pairs[1, p]].astype(jnp.float32)
            keep(p, a[1] * b[0] - a[0] * b[1])
            return 0

        lax.fori_loop(0, n - 1, arrive, 0)
        lax.fori_loop(0, n, power, 0, unroll=8)
        lax.fori_loop(0, npair, pair, 0, unroll=8)

        columns = []
        for c in range(chunks):
            x = rowsum[pl.ds(c, total, stride=group), :]
            for again in range(c + chunks, group, chunks):
                x += rowsum[pl.ds(again, total, stride=group), :]
            columns.append(x)
        high, low = split(jnp.concatenate(columns, axis=1))
        depth = chunks * LANES
        sums = jnp.dot(
            jnp.concatenate([high, low], axis=0),
            window[pl.ds(pl.multiple_of(q * depth, depth), depth), :],
            preferred_element_type=jnp.float32,
        )
        return looked + sums[:total] + sums[total:]

    looked = jnp.zeros((total, window.shape[1]), jnp.float32)
    looked = lax.fori_loop(0, pieces, piece_of, looked)

    def exact(left, x):
        width = x.shape[1]
        both = jnp.concatenate(split(x), axis=1)
        y = jnp.dot(left, both, preferred_element_type=jnp.float32)
        return y[:, :width] + y[:, width:]

    powers = exact(hot[...], looked[npair:])
    proxy = looked[:npair] * lax.rsqrt(powers[:npair] * powers[npair:] + 1e-06)
    out_ref[...] = exact(inverse[...], proxy).reshape(out_ref.shape)

    def left(k, _):
        for q in range(pieces):
            remote(q, (me + k) % n, me).wait_send()
        return 0

    lax.fori_loop(1, n, left, 0)


def per_device(n, slc, pairs, inverse):
    _, _, rows, cols = slc.shape
    steps, npair = inverse.shape
    pieces = PIECES
    chunks = cols // LANES // pieces
    span = LOOK_R * chunks
    group = max(chunks, 8)
    windows = cols // LOOK_C
    return pl.pallas_call(
        functools.partial(kernel, n, pieces),
        out_shape=pltpu.VMEM((steps, 1, windows), jnp.float32),
        in_specs=[pl.BlockSpec(memory_space=pltpu.HBM)] * 3,
        out_specs=pl.BlockSpec(memory_space=pltpu.VMEM),
        scratch_shapes=[
            pltpu.VMEM((2, rows, cols), jnp.bfloat16),
            pltpu.SMEM((2, npair), jnp.int32),
            pltpu.VMEM((2, npair), jnp.int32),
            pltpu.VMEM((steps, npair), jnp.bfloat16),
            pltpu.VMEM((pieces, 2, BLOCK * chunks, LANES), jnp.float32),
            pltpu.VMEM((pieces, n, 2, span, LANES), jnp.bfloat16),
            pltpu.VMEM((pieces, n, 2, span, LANES), jnp.bfloat16),
            pltpu.VMEM((n, 2, span, LANES), jnp.bfloat16),
            pltpu.VMEM(((npair + n) * group, LANES), jnp.float32),
            pltpu.VMEM((cols, windows), jnp.bfloat16),
            pltpu.VMEM((2 * npair, n), jnp.bfloat16),
            pltpu.SemaphoreType.DMA((rows // BLOCK,)),
            pltpu.SemaphoreType.DMA((3,)),
            pltpu.SemaphoreType.DMA((pieces, n)),
            pltpu.SemaphoreType.DMA((pieces, n)),
        ],
        compiler_params=pltpu.CompilerParams(
            collective_id=0, has_side_effects=True, vmem_limit_bytes=63 * 1024 * 1024
        ),
    )(slc, pairs.T, inverse)


def solution(mesh):
    n = mesh.shape["date"]
    in_specs = (P("date", None, "grp", None), P(), P())
    out_specs = P(None, ("grp", "date"), None)
    return jax.shard_map(
        functools.partial(per_device, n),
        mesh=mesh,
        in_specs=in_specs,
        out_specs=out_specs,
        check_vma=False,
    )
```

```python
import functools

import jax
import jax.numpy as jnp
from jax import lax
from jax.experimental import pallas as pl
from jax.experimental.pallas import tpu as pltpu
from jax.sharding import PartitionSpec as P

LOOK_R = 4
LOOK_C = 16
LANES = 128
BLOCK = 16
PIECES = 2


def split(x):
    high = x.astype(jnp.bfloat16)
    low = (x - high.astype(jnp.float32)).astype(jnp.bfloat16)
    return high, low


def kernel(
    n,
    pieces,
    slc_hbm,
    pairs_hbm,
    inverse_hbm,
    out_ref,
    tile,
    pairs,
    pairs_v,
    inverse,
    stage,
    send,
    recv,
    held,
    rowsum,
    window,
    hot,
    in_sem,
    small_sem,
    send_sem,
    recv_sem,
):
    me = lax.axis_index("date")
    half = n // 2
    rows, cols = tile.shape[1], tile.shape[2]
    chunks = cols // LANES // pieces
    span = LOOK_R * chunks
    blocks = rows // BLOCK
    near = blocks // 2
    per = BLOCK // LOOK_R
    npair = pairs.shape[1]
    total = npair + n
    group = rowsum.shape[0] // total
    base = (me // half) * half
    other = half - base
    block_base = (me // half) * near

    phase = (me // per) % 2

    def block_at(k):
        turn = k // 2
        far = jnp.where(me < half, blocks - 1 - turn, turn)
        own = block_base + (me // per + 1 + turn) % near
        return jnp.where((k + phase) % 2 == 0, far, own)

    def load(k):
        at = pl.ds(pl.multiple_of(block_at(k) * BLOCK, BLOCK), BLOCK)
        return pltpu.make_async_copy(
            slc_hbm.at[0, :, at, :], tile.at[:, at, :], in_sem.at[k]
        )

    smalls = [
        pltpu.make_async_copy(pairs_hbm, pairs, small_sem.at[0]),
        pltpu.make_async_copy(pairs_hbm, pairs_v, small_sem.at[1]),
        pltpu.make_async_copy(inverse_hbm, inverse, small_sem.at[2]),
    ]
    barrier = pltpu.get_barrier_semaphore()

    for k in [*range(half, n), *range(1, half)]:
        pl.semaphore_signal(
            barrier,
            inc=1,
            device_id={"date": (me + k) % n},
            device_id_type=pl.DeviceIdType.MESH,
        )
    for k in range(blocks):
        load(k).start()
    for copy in smalls:
        copy.start()

    def regroup(k):
        block = block_at(k)
        at = pl.ds(pl.multiple_of(block * BLOCK, BLOCK), BLOCK)
        for q in range(pieces):
            for part in range(2):
                for c in range(chunks):
                    column = (q * chunks + c) * LANES
                    piece = tile[part, at, column : column + LANES].astype(jnp.float32)
                    stage[q, part, pl.ds(c, BLOCK, stride=chunks), :] = piece
            for j in range(per):
                send[q, block * per + j] = stage[
                    q, :, j * span : (j + 1) * span, :
                ].astype(jnp.bfloat16)

    def remote(q, to, came):
        return pltpu.make_async_remote_copy(
            src_ref=send.at[q, to],
            dst_ref=recv.at[q, came],
            send_sem=send_sem.at[q, to],
            recv_sem=recv_sem.at[q, came],
            device_id={"date": to},
            device_id_type=pl.DeviceIdType.MESH,
        )

    def post(q, k):
        block = block_at(k)
        for j in range(per):
            to = block * per + (me + j) % per

            @pl.when(to != me)
            def _():
                remote(q, to, me).start()

    def fill(k, _):
        load(k).wait()
        regroup(k)

        @pl.when(k == 0)
        def _():
            pl.semaphore_wait(barrier, n - 1)

        post(0, k)
        return 0

    lax.fori_loop(0, blocks, fill, 0)

    def more(k, _):
        post(1 + k // blocks, k % blocks)
        return 0

    lax.fori_loop(0, (pieces - 1) * blocks, more, 0)

    for copy in smalls:
        copy.wait()

    def tile_of_window(c, _):
        shape = (LANES, window.shape[1])
        col = c * (LANES // LOOK_C) + lax.broadcasted_iota(jnp.int32, shape, 0) // LOOK_C
        win = lax.broadcasted_iota(jnp.int32, shape, 1)
        at = pl.ds(pl.multiple_of(c * LANES, LANES), LANES)
        window[at, :] = jnp.where(col == win, 1.0, 0.0).astype(jnp.bfloat16)
        return 0

    lax.fori_loop(0, cols // LANES, tile_of_window, 0)
    date = lax.broadcasted_iota(jnp.int32, (n, npair), 0)
    for which in range(2):
        flag = jnp.where(pairs_v[which : which + 1, :] == date, 1.0, 0.0)
        hot[which * npair : (which + 1) * npair, :] = flag.T.astype(jnp.bfloat16)
    for q in range(pieces):
        recv[q, me] = send[q, me]

    def keep(row, x):
        at = pl.ds(pl.multiple_of(row * group, group), group)
        rowsum[at, :] = x.reshape(-1, group, LANES).sum(axis=0)

    def piece_of(q, looked):
        def arrive(k, _):
            source = jnp.where(
                k < half, other + (me + k) % half, base + (me + k + 1) % half
            )
            remote(q, source, source).wait_recv()
            return 0

        def power(t, _):
            held[t] = recv[q, t]
            x = recv[q, t].astype(jnp.float32)
            keep(npair + t, x[0] * x[0] + x[1] * x[1])
            return 0

        def pair(p, _):
            a = held[pairs[0, p]].astype(jnp.float32)
            b = held[pairs[1, p]].astype(jnp.float32)
            keep(p, a[1] * b[0] - a[0] * b[1])
            return 0

        lax.fori_loop(0, n - 1, arrive, 0)
        lax.fori_loop(0, n, power, 0, unroll=8)
        lax.fori_loop(0, npair, pair, 0, unroll=8)

        columns = []
        for c in range(chunks):
            x = rowsum[pl.ds(c, total, stride=group), :]
            for again in range(c + chunks, group, chunks):
                x += rowsum[pl.ds(again, total, stride=group), :]
            columns.append(x)
        high, low = split(jnp.concatenate(columns, axis=1))
        depth = chunks * LANES
        sums = jnp.dot(
            jnp.concatenate([high, low], axis=0),
            window[pl.ds(pl.multiple_of(q * depth, depth), depth), :],
            preferred_element_type=jnp.float32,
        )
        return looked + sums[:total] + sums[total:]

    looked = jnp.zeros((total, window.shape[1]), jnp.float32)
    looked = lax.fori_loop(0, pieces, piece_of, looked)

    def exact(left, x):
        width = x.shape[1]
        both = jnp.concatenate(split(x), axis=1)
        y = jnp.dot(left, both, preferred_element_type=jnp.float32)
        return y[:, :width] + y[:, width:]

    powers = exact(hot[...], looked[npair:])
    proxy = looked[:npair] * lax.rsqrt(powers[:npair] * powers[npair:] + 1e-06)
    out_ref[...] = exact(inverse[...], proxy).reshape(out_ref.shape)

    def left(k, _):
        for q in range(pieces):
            remote(q, (me + k) % n, me).wait_send()
        return 0

    lax.fori_loop(1, n, left, 0)


def per_device(n, slc, pairs, inverse):
    _, _, rows, cols = slc.shape
    steps, npair = inverse.shape
    pieces = PIECES
    chunks = cols // LANES // pieces
    span = LOOK_R * chunks
    group = max(chunks, 8)
    windows = cols // LOOK_C
    return pl.pallas_call(
        functools.partial(kernel, n, pieces),
        out_shape=pltpu.VMEM((steps, 1, windows), jnp.float32),
        in_specs=[pl.BlockSpec(memory_space=pltpu.HBM)] * 3,
        out_specs=pl.BlockSpec(memory_space=pltpu.VMEM),
        scratch_shapes=[
            pltpu.VMEM((2, rows, cols), jnp.bfloat16),
            pltpu.SMEM((2, npair), jnp.int32),
            pltpu.VMEM((2, npair), jnp.int32),
            pltpu.VMEM((steps, npair), jnp.bfloat16),
            pltpu.VMEM((pieces, 2, BLOCK * chunks, LANES), jnp.float32),
            pltpu.VMEM((pieces, n, 2, span, LANES), jnp.bfloat16),
            pltpu.VMEM((pieces, n, 2, span, LANES), jnp.bfloat16),
            pltpu.VMEM((n, 2, span, LANES), jnp.bfloat16),
            pltpu.VMEM(((npair + n) * group, LANES), jnp.float32),
            pltpu.VMEM((cols, windows), jnp.bfloat16),
            pltpu.VMEM((2 * npair, n), jnp.bfloat16),
            pltpu.SemaphoreType.DMA((rows // BLOCK,)),
            pltpu.SemaphoreType.DMA((3,)),
            pltpu.SemaphoreType.DMA((pieces, n)),
            pltpu.SemaphoreType.DMA((pieces, n)),
        ],
        compiler_params=pltpu.CompilerParams(
            collective_id=0, has_side_effects=True, vmem_limit_bytes=63 * 1024 * 1024
        ),
    )(slc, pairs.T, inverse)


def solution(mesh):
    n = mesh.shape["date"]
    in_specs = (P("date", None, "grp", None), P(), P())
    out_specs = P(None, ("grp", "date"), None)
    return jax.shard_map(
        functools.partial(per_device, n),
        mesh=mesh,
        in_specs=in_specs,
        out_specs=out_specs,
        check_vma=False,
    )
```

```python
import functools

import jax
import jax.numpy as jnp
from jax import lax
from jax.experimental import pallas as pl
from jax.experimental.pallas import tpu as pltpu
from jax.sharding import PartitionSpec as P

LOOK_R = 4
LOOK_C = 16
LANES = 128
BLOCK = 16
PIECES = 4


def split(x):
    high = x.astype(jnp.bfloat16)
    low = (x - high.astype(jnp.float32)).astype(jnp.bfloat16)
    return high, low


def kernel(
    n,
    pieces,
    slc_hbm,
    pairs_hbm,
    inverse_hbm,
    out_ref,
    tile,
    pairs,
    pairs_v,
    inverse,
    stage,
    send,
    recv,
    held,
    rowsum,
    window,
    hot,
    in_sem,
    small_sem,
    send_sem,
    recv_sem,
):
    me = lax.axis_index("date")
    half = n // 2
    rows, cols = tile.shape[1], tile.shape[2]
    chunks = cols // LANES // pieces
    span = LOOK_R * chunks
    blocks = rows // BLOCK
    near = blocks // 2
    per = BLOCK // LOOK_R
    npair = pairs.shape[1]
    total = npair + n
    group = rowsum.shape[0] // total
    base = (me // half) * half
    other = half - base
    block_base = (me // half) * near

    phase = (me // per) % 2

    def block_at(k):
        turn = k // 2
        far = jnp.where(me < half, blocks - 1 - turn, turn)
        own = block_base + (me // per + 1 + turn) % near
        return jnp.where((k + phase) % 2 == 0, far, own)

    def load(k):
        at = pl.ds(pl.multiple_of(block_at(k) * BLOCK, BLOCK), BLOCK)
        return pltpu.make_async_copy(
            slc_hbm.at[0, :, at, :], tile.at[:, at, :], in_sem.at[k]
        )

    smalls = [
        pltpu.make_async_copy(pairs_hbm, pairs, small_sem.at[0]),
        pltpu.make_async_copy(pairs_hbm, pairs_v, small_sem.at[1]),
        pltpu.make_async_copy(inverse_hbm, inverse, small_sem.at[2]),
    ]
    barrier = pltpu.get_barrier_semaphore()

    for k in [*range(half, n), *range(1, half)]:
        pl.semaphore_signal(
            barrier,
            inc=1,
            device_id={"date": (me + k) % n},
            device_id_type=pl.DeviceIdType.MESH,
        )
    for k in range(blocks):
        load(k).start()
    for copy in smalls:
        copy.start()

    def regroup(k):
        block = block_at(k)
        at = pl.ds(pl.multiple_of(block * BLOCK, BLOCK), BLOCK)
        for q in range(pieces):
            for part in range(2):
                for c in range(chunks):
                    column = (q * chunks + c) * LANES
                    piece = tile[part, at, column : column + LANES].astype(jnp.float32)
                    stage[q, part, pl.ds(c, BLOCK, stride=chunks), :] = piece
            for j in range(per):
                send[q, block * per + j] = stage[
                    q, :, j * span : (j + 1) * span, :
                ].astype(jnp.bfloat16)

    def remote(q, to, came):
        return pltpu.make_async_remote_copy(
            src_ref=send.at[q, to],
            dst_ref=recv.at[q, came],
            send_sem=send_sem.at[q, to],
            recv_sem=recv_sem.at[q, came],
            device_id={"date": to},
            device_id_type=pl.DeviceIdType.MESH,
        )

    def post(q, k):
        block = block_at(k)
        for j in range(per):
            to = block * per + (me + j) % per

            @pl.when(to != me)
            def _():
                remote(q, to, me).start()

    def fill(k, _):
        load(k).wait()
        regroup(k)

        @pl.when(k == 0)
        def _():
            pl.semaphore_wait(barrier, n - 1)

        post(0, k)
        return 0

    lax.fori_loop(0, blocks, fill, 0)

    def more(k, _):
        post(1 + k // blocks, k % blocks)
        return 0

    lax.fori_loop(0, (pieces - 1) * blocks, more, 0)

    for copy in smalls:
        copy.wait()

    def tile_of_window(c, _):
        shape = (LANES, window.shape[1])
        col = c * (LANES // LOOK_C) + lax.broadcasted_iota(jnp.int32, shape, 0) // LOOK_C
        win = lax.broadcasted_iota(jnp.int32, shape, 1)
        at = pl.ds(pl.multiple_of(c * LANES, LANES), LANES)
        window[at, :] = jnp.where(col == win, 1.0, 0.0).astype(jnp.bfloat16)
        return 0

    lax.fori_loop(0, cols // LANES, tile_of_window, 0)
    date = lax.broadcasted_iota(jnp.int32, (n, npair), 0)
    for which in range(2):
        flag = jnp.where(pairs_v[which : which + 1, :] == date, 1.0, 0.0)
        hot[which * npair : (which + 1) * npair, :] = flag.T.astype(jnp.bfloat16)
    for q in range(pieces):
        recv[q, me] = send[q, me]

    def keep(row, x):
        at = pl.ds(pl.multiple_of(row * group, group), group)
        rowsum[at, :] = x.reshape(-1, group, LANES).sum(axis=0)

    def piece_of(q, looked):
        def arrive(k, _):
            source = jnp.where(
                k < half, other + (me + k) % half, base + (me + k + 1) % half
            )
            remote(q, source, source).wait_recv()
            return 0

        def power(t, _):
            held[t] = recv[q, t]
            x = recv[q, t].astype(jnp.float32)
            keep(npair + t, x[0] * x[0] + x[1] * x[1])
            return 0

        def pair(p, _):
            a = held[pairs[0, p]].astype(jnp.float32)
            b = held[pairs[1, p]].astype(jnp.float32)
            keep(p, a[1] * b[0] - a[0] * b[1])
            return 0

        lax.fori_loop(0, n - 1, arrive, 0)
        lax.fori_loop(0, n, power, 0, unroll=8)
        lax.fori_loop(0, npair, pair, 0, unroll=8)

        columns = []
        for c in range(chunks):
            x = rowsum[pl.ds(c, total, stride=group), :]
            for again in range(c + chunks, group, chunks):
                x += rowsum[pl.ds(again, total, stride=group), :]
            columns.append(x)
        high, low = split(jnp.concatenate(columns, axis=1))
        depth = chunks * LANES
        sums = jnp.dot(
            jnp.concatenate([high, low], axis=0),
            window[pl.ds(pl.multiple_of(q * depth, depth), depth), :],
            preferred_element_type=jnp.float32,
        )
        return looked + sums[:total] + sums[total:]

    looked = jnp.zeros((total, window.shape[1]), jnp.float32)
    looked = lax.fori_loop(0, pieces, piece_of, looked)

    def exact(left, x):
        width = x.shape[1]
        both = jnp.concatenate(split(x), axis=1)
        y = jnp.dot(left, both, preferred_element_type=jnp.float32)
        return y[:, :width] + y[:, width:]

    powers = exact(hot[...], looked[npair:])
    proxy = looked[:npair] * lax.rsqrt(powers[:npair] * powers[npair:] + 1e-06)
    out_ref[...] = exact(inverse[...], proxy).reshape(out_ref.shape)

    def left(k, _):
        for q in range(pieces):
            remote(q, (me + k) % n, me).wait_send()
        return 0

    lax.fori_loop(1, n, left, 0)


def per_device(n, slc, pairs, inverse):
    _, _, rows, cols = slc.shape
    steps, npair = inverse.shape
    pieces = PIECES
    chunks = cols // LANES // pieces
    span = LOOK_R * chunks
    group = max(chunks, 8)
    windows = cols // LOOK_C
    return pl.pallas_call(
        functools.partial(kernel, n, pieces),
        out_shape=pltpu.VMEM((steps, 1, windows), jnp.float32),
        in_specs=[pl.BlockSpec(memory_space=pltpu.HBM)] * 3,
        out_specs=pl.BlockSpec(memory_space=pltpu.VMEM),
        scratch_shapes=[
            pltpu.VMEM((2, rows, cols), jnp.bfloat16),
            pltpu.SMEM((2, npair), jnp.int32),
            pltpu.VMEM((2, npair), jnp.int32),
            pltpu.VMEM((steps, npair), jnp.bfloat16),
            pltpu.VMEM((pieces, 2, BLOCK * chunks, LANES), jnp.float32),
            pltpu.VMEM((pieces, n, 2, span, LANES), jnp.bfloat16),
            pltpu.VMEM((pieces, n, 2, span, LANES), jnp.bfloat16),
            pltpu.VMEM((n, 2, span, LANES), jnp.bfloat16),
            pltpu.VMEM(((npair + n) * group, LANES), jnp.float32),
            pltpu.VMEM((cols, windows), jnp.bfloat16),
            pltpu.VMEM((2 * npair, n), jnp.bfloat16),
            pltpu.SemaphoreType.DMA((rows // BLOCK,)),
            pltpu.SemaphoreType.DMA((3,)),
            pltpu.SemaphoreType.DMA((pieces, n)),
            pltpu.SemaphoreType.DMA((pieces, n)),
        ],
        compiler_params=pltpu.CompilerParams(
            collective_id=0, has_side_effects=True, vmem_limit_bytes=63 * 1024 * 1024
        ),
    )(slc, pairs.T, inverse)


def solution(mesh):
    n = mesh.shape["date"]
    in_specs = (P("date", None, "grp", None), P(), P())
    out_specs = P(None, ("grp", "date"), None)
    return jax.shard_map(
        functools.partial(per_device, n),
        mesh=mesh,
        in_specs=in_specs,
        out_specs=out_specs,
        check_vma=False,
    )
```

```python
import functools

import jax
import jax.numpy as jnp
from jax import lax
from jax.experimental import pallas as pl
from jax.experimental.pallas import tpu as pltpu
from jax.sharding import PartitionSpec as P

LOOK_R = 4
LOOK_C = 16
LANES = 128
BLOCK = 16
PIECES = 2


def split(x):
    high = x.astype(jnp.bfloat16)
    low = (x - high.astype(jnp.float32)).astype(jnp.bfloat16)
    return high, low


def kernel(
    n,
    pieces,
    slc_hbm,
    pairs_hbm,
    inverse_hbm,
    out_ref,
    tile,
    pairs,
    pairs_v,
    inverse,
    stage,
    send,
    recv,
    held,
    rowsum,
    window,
    hot,
    in_sem,
    small_sem,
    send_sem,
    recv_sem,
):
    me = lax.axis_index("date")
    half = n // 2
    rows, cols = tile.shape[1], tile.shape[2]
    chunks = cols // LANES // pieces
    span = LOOK_R * chunks
    blocks = rows // BLOCK
    near = blocks // 2
    per = BLOCK // LOOK_R
    npair = pairs.shape[1]
    total = npair + n
    group = rowsum.shape[0] // total
    base = (me // half) * half
    other = half - base
    block_base = (me // half) * near

    phase = (me // per) % 2

    def block_at(k):
        turn = k // 2
        far = jnp.where(me < half, blocks - 1 - turn, turn)
        own = block_base + (me // per + 1 + turn) % near
        return jnp.where((k + phase) % 2 == 0, far, own)

    def load(k):
        at = pl.ds(pl.multiple_of(block_at(k) * BLOCK, BLOCK), BLOCK)
        return pltpu.make_async_copy(
            slc_hbm.at[0, :, at, :], tile.at[:, at, :], in_sem.at[k]
        )

    smalls = [
        pltpu.make_async_copy(pairs_hbm, pairs, small_sem.at[0]),
        pltpu.make_async_copy(pairs_hbm, pairs_v, small_sem.at[1]),
        pltpu.make_async_copy(inverse_hbm, inverse, small_sem.at[2]),
    ]
    barrier = pltpu.get_barrier_semaphore()

    for k in [*range(half, n), *range(1, half)]:
        pl.semaphore_signal(
            barrier,
            inc=1,
            device_id={"date": (me + k) % n},
            device_id_type=pl.DeviceIdType.MESH,
        )
    for k in range(blocks):
        load(k).start()
    for copy in smalls:
        copy.start()

    def regroup(k):
        block = block_at(k)
        at = pl.ds(pl.multiple_of(block * BLOCK, BLOCK), BLOCK)
        for q in range(pieces):
            for part in range(2):
                for c in range(chunks):
                    column = (q * chunks + c) * LANES
                    piece = tile[part, at, column : column + LANES].astype(jnp.float32)
                    stage[q, part, pl.ds(c, BLOCK, stride=chunks), :] = piece
            for j in range(per):
                send[q, block * per + j] = stage[
                    q, :, j * span : (j + 1) * span, :
                ].astype(jnp.bfloat16)

    def remote(q, to, came):
        return pltpu.make_async_remote_copy(
            src_ref=send.at[q, to],
            dst_ref=recv.at[q, came],
            send_sem=send_sem.at[q],
            recv_sem=recv_sem.at[q],
            device_id={"date": to},
            device_id_type=pl.DeviceIdType.MESH,
        )

    def every(q):
        return pltpu.make_async_remote_copy(
            src_ref=send.at[q, pl.ds(0, n - 1)],
            dst_ref=recv.at[q, pl.ds(0, n - 1)],
            send_sem=send_sem.at[q],
            recv_sem=recv_sem.at[q],
            device_id={"date": (me + 1) % n},
            device_id_type=pl.DeviceIdType.MESH,
        )

    def post(q, k):
        block = block_at(k)
        for j in range(per):
            to = block * per + (me + j) % per

            @pl.when(to != me)
            def _():
                remote(q, to, me).start()

    def fill(k, _):
        load(k).wait()
        regroup(k)

        @pl.when(k == 0)
        def _():
            pl.semaphore_wait(barrier, n - 1)

        post(0, k)
        return 0

    lax.fori_loop(0, blocks, fill, 0)

    def more(k, _):
        post(1 + k // blocks, k % blocks)
        return 0

    lax.fori_loop(0, (pieces - 1) * blocks, more, 0)

    for copy in smalls:
        copy.wait()

    def tile_of_window(c, _):
        shape = (LANES, window.shape[1])
        col = c * (LANES // LOOK_C) + lax.broadcasted_iota(jnp.int32, shape, 0) // LOOK_C
        win = lax.broadcasted_iota(jnp.int32, shape, 1)
        at = pl.ds(pl.multiple_of(c * LANES, LANES), LANES)
        window[at, :] = jnp.where(col == win, 1.0, 0.0).astype(jnp.bfloat16)
        return 0

    lax.fori_loop(0, cols // LANES, tile_of_window, 0)
    date = lax.broadcasted_iota(jnp.int32, (n, npair), 0)
    for which in range(2):
        flag = jnp.where(pairs_v[which : which + 1, :] == date, 1.0, 0.0)
        hot[which * npair : (which + 1) * npair, :] = flag.T.astype(jnp.bfloat16)
    for q in range(pieces):
        recv[q, me] = send[q, me]

    def keep(row, x):
        at = pl.ds(pl.multiple_of(row * group, group), group)
        rowsum[at, :] = x.reshape(-1, group, LANES).sum(axis=0)

    def piece_of(q, looked):
        def power(t, _):
            held[t] = recv[q, t]
            x = recv[q, t].astype(jnp.float32)
            keep(npair + t, x[0] * x[0] + x[1] * x[1])
            return 0

        def pair(p, _):
            a = held[pairs[0, p]].astype(jnp.float32)
            b = held[pairs[1, p]].astype(jnp.float32)
            keep(p, a[1] * b[0] - a[0] * b[1])
            return 0

        every(q).wait_recv()
        lax.fori_loop(0, n, power, 0, unroll=8)
        lax.fori_loop(0, npair, pair, 0, unroll=8)

        columns = []
        for c in range(chunks):
            x = rowsum[pl.ds(c, total, stride=group), :]
            for again in range(c + chunks, group, chunks):
                x += rowsum[pl.ds(again, total, stride=group), :]
            columns.append(x)
        high, low = split(jnp.concatenate(columns, axis=1))
        depth = chunks * LANES
        sums = jnp.dot(
            jnp.concatenate([high, low], axis=0),
            window[pl.ds(pl.multiple_of(q * depth, depth), depth), :],
            preferred_element_type=jnp.float32,
        )
        return looked + sums[:total] + sums[total:]

    looked = jnp.zeros((total, window.shape[1]), jnp.float32)
    looked = lax.fori_loop(0, pieces, piece_of, looked)

    def exact(left, x):
        width = x.shape[1]
        both = jnp.concatenate(split(x), axis=1)
        y = jnp.dot(left, both, preferred_element_type=jnp.float32)
        return y[:, :width] + y[:, width:]

    powers = exact(hot[...], looked[npair:])
    proxy = looked[:npair] * lax.rsqrt(powers[:npair] * powers[npair:] + 1e-06)
    out_ref[...] = exact(inverse[...], proxy).reshape(out_ref.shape)

    for q in range(pieces):
        every(q).wait_send()


def per_device(n, slc, pairs, inverse):
    _, _, rows, cols = slc.shape
    steps, npair = inverse.shape
    pieces = PIECES
    chunks = cols // LANES // pieces
    span = LOOK_R * chunks
    group = max(chunks, 8)
    windows = cols // LOOK_C
    return pl.pallas_call(
        functools.partial(kernel, n, pieces),
        out_shape=pltpu.VMEM((steps, 1, windows), jnp.float32),
        in_specs=[pl.BlockSpec(memory_space=pltpu.HBM)] * 3,
        out_specs=pl.BlockSpec(memory_space=pltpu.VMEM),
        scratch_shapes=[
            pltpu.VMEM((2, rows, cols), jnp.bfloat16),
            pltpu.SMEM((2, npair), jnp.int32),
            pltpu.VMEM((2, npair), jnp.int32),
            pltpu.VMEM((steps, npair), jnp.bfloat16),
            pltpu.VMEM((pieces, 2, BLOCK * chunks, LANES), jnp.float32),
            pltpu.VMEM((pieces, n, 2, span, LANES), jnp.bfloat16),
            pltpu.VMEM((pieces, n, 2, span, LANES), jnp.bfloat16),
            pltpu.VMEM((n, 2, span, LANES), jnp.bfloat16),
            pltpu.VMEM(((npair + n) * group, LANES), jnp.float32),
            pltpu.VMEM((cols, windows), jnp.bfloat16),
            pltpu.VMEM((2 * npair, n), jnp.bfloat16),
            pltpu.SemaphoreType.DMA((rows // BLOCK,)),
            pltpu.SemaphoreType.DMA((3,)),
            pltpu.SemaphoreType.DMA((pieces,)),
            pltpu.SemaphoreType.DMA((pieces,)),
        ],
        compiler_params=pltpu.CompilerParams(
            collective_id=0, has_side_effects=True, vmem_limit_bytes=63 * 1024 * 1024
        ),
    )(slc, pairs.T, inverse)


def solution(mesh):
    n = mesh.shape["date"]
    in_specs = (P("date", None, "grp", None), P(), P())
    out_specs = P(None, ("grp", "date"), None)
    return jax.shard_map(
        functools.partial(per_device, n),
        mesh=mesh,
        in_specs=in_specs,
        out_specs=out_specs,
        check_vma=False,
    )
```

```python
import functools

import jax
import jax.numpy as jnp
from jax import lax
from jax.experimental import pallas as pl
from jax.experimental.pallas import tpu as pltpu
from jax.sharding import PartitionSpec as P

LOOK_R = 4
LOOK_C = 16
LANES = 128
BLOCK = 16
PIECES = 2


def split(x):
    high = x.astype(jnp.bfloat16)
    low = (x - high.astype(jnp.float32)).astype(jnp.bfloat16)
    return high, low


def kernel(
    n,
    pieces,
    slc_hbm,
    pairs_hbm,
    inverse_hbm,
    out_ref,
    tile,
    pairs,
    pairs_v,
    inverse,
    stage,
    send,
    recv,
    held,
    rowsum,
    window,
    hot,
    in_sem,
    small_sem,
    send_sem,
    recv_sem,
):
    me = lax.axis_index("date")
    half = n // 2
    rows, cols = tile.shape[1], tile.shape[2]
    chunks = cols // LANES // pieces
    span = LOOK_R * chunks
    blocks = rows // BLOCK
    near = blocks // 2
    per = BLOCK // LOOK_R
    npair = pairs.shape[1]
    total = npair + n
    group = rowsum.shape[0] // total
    base = (me // half) * half
    other = half - base
    block_base = (me // half) * near

    phase = (me // per) % 2

    def block_at(k):
        turn = k // 2
        far = jnp.where(me < half, blocks - 1 - turn, turn)
        own = block_base + (me // per + 1 + turn) % near
        return jnp.where((k + phase) % 2 == 0, far, own)

    def load(k):
        at = pl.ds(pl.multiple_of(block_at(k) * BLOCK, BLOCK), BLOCK)
        return pltpu.make_async_copy(
            slc_hbm.at[0, :, at, :], tile.at[:, at, :], in_sem.at[k]
        )

    smalls = [
        pltpu.make_async_copy(pairs_hbm, pairs, small_sem.at[0]),
        pltpu.make_async_copy(pairs_hbm, pairs_v, small_sem.at[1]),
        pltpu.make_async_copy(inverse_hbm, inverse, small_sem.at[2]),
    ]
    barrier = pltpu.get_barrier_semaphore()

    for k in [*range(half, n), *range(1, half)]:
        pl.semaphore_signal(
            barrier,
            inc=1,
            device_id={"date": (me + k) % n},
            device_id_type=pl.DeviceIdType.MESH,
        )
    for k in range(blocks):
        load(k).start()
    for copy in smalls:
        copy.start()

    def regroup(k):
        block = block_at(k)
        at = pl.ds(pl.multiple_of(block * BLOCK, BLOCK), BLOCK)
        for q in range(pieces):
            for part in range(2):
                for c in range(chunks):
                    column = (q * chunks + c) * LANES
                    piece = tile[part, at, column : column + LANES].astype(jnp.float32)
                    stage[q, part, pl.ds(c, BLOCK, stride=chunks), :] = piece
            for j in range(per):
                send[q, block * per + j] = stage[
                    q, :, j * span : (j + 1) * span, :
                ].astype(jnp.bfloat16)

    def remote(q, to, came):
        return pltpu.make_async_remote_copy(
            src_ref=send.at[q, to],
            dst_ref=recv.at[q, came],
            send_sem=send_sem.at[q],
            recv_sem=recv_sem.at[q],
            device_id={"date": to},
            device_id_type=pl.DeviceIdType.MESH,
        )

    def every(q):
        return pltpu.make_async_remote_copy(
            src_ref=send.at[q, pl.ds(0, n - 1)],
            dst_ref=recv.at[q, pl.ds(0, n - 1)],
            send_sem=send_sem.at[q],
            recv_sem=recv_sem.at[q],
            device_id={"date": (me + 1) % n},
            device_id_type=pl.DeviceIdType.MESH,
        )

    def post(q, k):
        block = block_at(k)
        for j in range(per):
            to = block * per + (me + j) % per

            @pl.when(to != me)
            def _():
                remote(q, to, me).start()

    def fill(k, _):
        load(k).wait()
        regroup(k)

        @pl.when(k == 0)
        def _():
            pl.semaphore_wait(barrier, n - 1)

        post(0, k)
        return 0

    lax.fori_loop(0, blocks, fill, 0)

    def more(k, _):
        post(1 + k // blocks, k % blocks)
        return 0

    lax.fori_loop(0, (pieces - 1) * blocks, more, 0)

    for copy in smalls:
        copy.wait()

    def tile_of_window(c, _):
        shape = (LANES, window.shape[1])
        col = c * (LANES // LOOK_C) + lax.broadcasted_iota(jnp.int32, shape, 0) // LOOK_C
        win = lax.broadcasted_iota(jnp.int32, shape, 1)
        at = pl.ds(pl.multiple_of(c * LANES, LANES), LANES)
        window[at, :] = jnp.where(col == win, 1.0, 0.0).astype(jnp.bfloat16)
        return 0

    lax.fori_loop(0, cols // LANES, tile_of_window, 0)
    date = lax.broadcasted_iota(jnp.int32, (n, npair), 0)
    for which in range(2):
        flag = jnp.where(pairs_v[which : which + 1, :] == date, 1.0, 0.0)
        hot[which * npair : (which + 1) * npair, :] = flag.T.astype(jnp.bfloat16)
    for q in range(pieces):
        recv[q, me] = send[q, me]

    def keep(row, x):
        at = pl.ds(pl.multiple_of(row * group, group), group)
        rowsum[at, :] = x.reshape(-1, group, LANES).sum(axis=0)

    def piece_of(q, looked):
        def power(t, _):
            x = recv[q, t].astype(jnp.float32)
            held[t] = x
            keep(npair + t, x[0] * x[0] + x[1] * x[1])
            return 0

        def pair(p, _):
            a = held[pairs[0, p]]
            b = held[pairs[1, p]]
            keep(p, a[1] * b[0] - a[0] * b[1])
            return 0

        every(q).wait_recv()
        lax.fori_loop(0, n, power, 0, unroll=8)
        lax.fori_loop(0, npair, pair, 0, unroll=8)

        columns = []
        for c in range(chunks):
            x = rowsum[pl.ds(c, total, stride=group), :]
            for again in range(c + chunks, group, chunks):
                x += rowsum[pl.ds(again, total, stride=group), :]
            columns.append(x)
        high, low = split(jnp.concatenate(columns, axis=1))
        depth = chunks * LANES
        sums = jnp.dot(
            jnp.concatenate([high, low], axis=0),
            window[pl.ds(pl.multiple_of(q * depth, depth), depth), :],
            preferred_element_type=jnp.float32,
        )
        return looked + sums[:total] + sums[total:]

    looked = jnp.zeros((total, window.shape[1]), jnp.float32)
    looked = lax.fori_loop(0, pieces, piece_of, looked)

    def exact(left, x):
        width = x.shape[1]
        both = jnp.concatenate(split(x), axis=1)
        y = jnp.dot(left, both, preferred_element_type=jnp.float32)
        return y[:, :width] + y[:, width:]

    powers = exact(hot[...], looked[npair:])
    proxy = looked[:npair] * lax.rsqrt(powers[:npair] * powers[npair:] + 1e-06)
    out_ref[...] = exact(inverse[...], proxy).reshape(out_ref.shape)

    for q in range(pieces):
        every(q).wait_send()


def per_device(n, slc, pairs, inverse):
    _, _, rows, cols = slc.shape
    steps, npair = inverse.shape
    pieces = PIECES
    chunks = cols // LANES // pieces
    span = LOOK_R * chunks
    group = max(chunks, 8)
    windows = cols // LOOK_C
    return pl.pallas_call(
        functools.partial(kernel, n, pieces),
        out_shape=pltpu.VMEM((steps, 1, windows), jnp.float32),
        in_specs=[pl.BlockSpec(memory_space=pltpu.HBM)] * 3,
        out_specs=pl.BlockSpec(memory_space=pltpu.VMEM),
        scratch_shapes=[
            pltpu.VMEM((2, rows, cols), jnp.bfloat16),
            pltpu.SMEM((2, npair), jnp.int32),
            pltpu.VMEM((2, npair), jnp.int32),
            pltpu.VMEM((steps, npair), jnp.bfloat16),
            pltpu.VMEM((pieces, 2, BLOCK * chunks, LANES), jnp.float32),
            pltpu.VMEM((pieces, n, 2, span, LANES), jnp.bfloat16),
            pltpu.VMEM((pieces, n, 2, span, LANES), jnp.bfloat16),
            pltpu.VMEM((n, 2, span, LANES), jnp.float32),
            pltpu.VMEM(((npair + n) * group, LANES), jnp.float32),
            pltpu.VMEM((cols, windows), jnp.bfloat16),
            pltpu.VMEM((2 * npair, n), jnp.bfloat16),
            pltpu.SemaphoreType.DMA((rows // BLOCK,)),
            pltpu.SemaphoreType.DMA((3,)),
            pltpu.SemaphoreType.DMA((pieces,)),
            pltpu.SemaphoreType.DMA((pieces,)),
        ],
        compiler_params=pltpu.CompilerParams(
            collective_id=0, has_side_effects=True, vmem_limit_bytes=63 * 1024 * 1024
        ),
    )(slc, pairs.T, inverse)


def solution(mesh):
    n = mesh.shape["date"]
    in_specs = (P("date", None, "grp", None), P(), P())
    out_specs = P(None, ("grp", "date"), None)
    return jax.shard_map(
        functools.partial(per_device, n),
        mesh=mesh,
        in_specs=in_specs,
        out_specs=out_specs,
        check_vma=False,
    )
```

```python
import functools

import jax
import jax.numpy as jnp
from jax import lax
from jax.experimental import pallas as pl
from jax.experimental.pallas import tpu as pltpu
from jax.sharding import PartitionSpec as P

LOOK_R = 4
LOOK_C = 16
LANES = 128
BLOCK = 16
PIECES = 1


def split(x):
    high = x.astype(jnp.bfloat16)
    low = (x - high.astype(jnp.float32)).astype(jnp.bfloat16)
    return high, low


def kernel(
    n,
    pieces,
    slc_hbm,
    pairs_hbm,
    inverse_hbm,
    out_ref,
    tile,
    pairs,
    pairs_v,
    inverse,
    stage,
    send,
    recv,
    held,
    rowsum,
    window,
    hot,
    in_sem,
    small_sem,
    send_sem,
    recv_sem,
):
    me = lax.axis_index("date")
    half = n // 2
    rows, cols = tile.shape[1], tile.shape[2]
    chunks = cols // LANES // pieces
    span = LOOK_R * chunks
    blocks = rows // BLOCK
    near = blocks // 2
    per = BLOCK // LOOK_R
    npair = pairs.shape[1]
    total = npair + n
    group = rowsum.shape[0] // total
    base = (me // half) * half
    other = half - base
    block_base = (me // half) * near

    phase = (me // per) % 2

    def block_at(k):
        turn = k // 2
        far = jnp.where(me < half, blocks - 1 - turn, turn)
        own = block_base + (me // per + 1 + turn) % near
        return jnp.where((k + phase) % 2 == 0, far, own)

    def load(k):
        at = pl.ds(pl.multiple_of(block_at(k) * BLOCK, BLOCK), BLOCK)
        return pltpu.make_async_copy(
            slc_hbm.at[0, :, at, :], tile.at[:, at, :], in_sem.at[k]
        )

    smalls = [
        pltpu.make_async_copy(pairs_hbm, pairs, small_sem.at[0]),
        pltpu.make_async_copy(pairs_hbm, pairs_v, small_sem.at[1]),
        pltpu.make_async_copy(inverse_hbm, inverse, small_sem.at[2]),
    ]
    barrier = pltpu.get_barrier_semaphore()

    for k in [*range(half, n), *range(1, half)]:
        pl.semaphore_signal(
            barrier,
            inc=1,
            device_id={"date": (me + k) % n},
            device_id_type=pl.DeviceIdType.MESH,
        )
    for k in range(blocks):
        load(k).start()
    for copy in smalls:
        copy.start()

    def regroup(k):
        block = block_at(k)
        at = pl.ds(pl.multiple_of(block * BLOCK, BLOCK), BLOCK)
        for q in range(pieces):
            for part in range(2):
                for c in range(chunks):
                    column = (q * chunks + c) * LANES
                    piece = tile[part, at, column : column + LANES].astype(jnp.float32)
                    stage[q, part, pl.ds(c, BLOCK, stride=chunks), :] = piece
            for j in range(per):
                send[q, block * per + j] = stage[
                    q, :, j * span : (j + 1) * span, :
                ].astype(jnp.bfloat16)

    def remote(q, to, came):
        return pltpu.make_async_remote_copy(
            src_ref=send.at[q, to],
            dst_ref=recv.at[q, came],
            send_sem=send_sem.at[q],
            recv_sem=recv_sem.at[q],
            device_id={"date": to},
            device_id_type=pl.DeviceIdType.MESH,
        )

    def every(q):
        return pltpu.make_async_remote_copy(
            src_ref=send.at[q, pl.ds(0, n - 1)],
            dst_ref=recv.at[q, pl.ds(0, n - 1)],
            send_sem=send_sem.at[q],
            recv_sem=recv_sem.at[q],
            device_id={"date": (me + 1) % n},
            device_id_type=pl.DeviceIdType.MESH,
        )

    def post(q, k):
        block = block_at(k)
        for j in range(per):
            to = block * per + (me + j) % per

            @pl.when(to != me)
            def _():
                remote(q, to, me).start()

    def fill(k, _):
        load(k).wait()
        regroup(k)

        @pl.when(k == 0)
        def _():
            pl.semaphore_wait(barrier, n - 1)

        post(0, k)
        return 0

    lax.fori_loop(0, blocks, fill, 0)

    def more(k, _):
        post(1 + k // blocks, k % blocks)
        return 0

    lax.fori_loop(0, (pieces - 1) * blocks, more, 0)

    for copy in smalls:
        copy.wait()

    def tile_of_window(c, _):
        shape = (LANES, window.shape[1])
        col = c * (LANES // LOOK_C) + lax.broadcasted_iota(jnp.int32, shape, 0) // LOOK_C
        win = lax.broadcasted_iota(jnp.int32, shape, 1)
        at = pl.ds(pl.multiple_of(c * LANES, LANES), LANES)
        window[at, :] = jnp.where(col == win, 1.0, 0.0).astype(jnp.bfloat16)
        return 0

    lax.fori_loop(0, cols // LANES, tile_of_window, 0)
    date = lax.broadcasted_iota(jnp.int32, (n, npair), 0)
    for which in range(2):
        flag = jnp.where(pairs_v[which : which + 1, :] == date, 1.0, 0.0)
        hot[which * npair : (which + 1) * npair, :] = flag.T.astype(jnp.bfloat16)
    for q in range(pieces):
        recv[q, me] = send[q, me]

    def keep(row, x):
        at = pl.ds(pl.multiple_of(row * group, group), group)
        rowsum[at, :] = x.reshape(-1, group, LANES).sum(axis=0)

    def piece_of(q, looked):
        def power(t, _):
            x = recv[q, t].astype(jnp.float32)
            held[t] = x
            keep(npair + t, x[0] * x[0] + x[1] * x[1])
            return 0

        def pair(p, _):
            a = held[pairs[0, p]]
            b = held[pairs[1, p]]
            keep(p, a[1] * b[0] - a[0] * b[1])
            return 0

        every(q).wait_recv()
        lax.fori_loop(0, n, power, 0, unroll=8)
        lax.fori_loop(0, npair, pair, 0, unroll=8)

        columns = []
        for c in range(chunks):
            x = rowsum[pl.ds(c, total, stride=group), :]
            for again in range(c + chunks, group, chunks):
                x += rowsum[pl.ds(again, total, stride=group), :]
            columns.append(x)
        high, low = split(jnp.concatenate(columns, axis=1))
        depth = chunks * LANES
        sums = jnp.dot(
            jnp.concatenate([high, low], axis=0),
            window[pl.ds(pl.multiple_of(q * depth, depth), depth), :],
            preferred_element_type=jnp.float32,
        )
        return looked + sums[:total] + sums[total:]

    looked = jnp.zeros((total, window.shape[1]), jnp.float32)
    looked = lax.fori_loop(0, pieces, piece_of, looked)

    def exact(left, x):
        width = x.shape[1]
        both = jnp.concatenate(split(x), axis=1)
        y = jnp.dot(left, both, preferred_element_type=jnp.float32)
        return y[:, :width] + y[:, width:]

    powers = exact(hot[...], looked[npair:])
    proxy = looked[:npair] * lax.rsqrt(powers[:npair] * powers[npair:] + 1e-06)
    out_ref[...] = exact(inverse[...], proxy).reshape(out_ref.shape)

    for q in range(pieces):
        every(q).wait_send()


def per_device(n, slc, pairs, inverse):
    _, _, rows, cols = slc.shape
    steps, npair = inverse.shape
    pieces = PIECES
    chunks = cols // LANES // pieces
    span = LOOK_R * chunks
    group = max(chunks, 8)
    windows = cols // LOOK_C
    return pl.pallas_call(
        functools.partial(kernel, n, pieces),
        out_shape=pltpu.VMEM((steps, 1, windows), jnp.float32),
        in_specs=[pl.BlockSpec(memory_space=pltpu.HBM)] * 3,
        out_specs=pl.BlockSpec(memory_space=pltpu.VMEM),
        scratch_shapes=[
            pltpu.VMEM((2, rows, cols), jnp.bfloat16),
            pltpu.SMEM((2, npair), jnp.int32),
            pltpu.VMEM((2, npair), jnp.int32),
            pltpu.VMEM((steps, npair), jnp.bfloat16),
            pltpu.VMEM((pieces, 2, BLOCK * chunks, LANES), jnp.float32),
            pltpu.VMEM((pieces, n, 2, span, LANES), jnp.bfloat16),
            pltpu.VMEM((pieces, n, 2, span, LANES), jnp.bfloat16),
            pltpu.VMEM((n, 2, span, LANES), jnp.float32),
            pltpu.VMEM(((npair + n) * group, LANES), jnp.float32),
            pltpu.VMEM((cols, windows), jnp.bfloat16),
            pltpu.VMEM((2 * npair, n), jnp.bfloat16),
            pltpu.SemaphoreType.DMA((rows // BLOCK,)),
            pltpu.SemaphoreType.DMA((3,)),
            pltpu.SemaphoreType.DMA((pieces,)),
            pltpu.SemaphoreType.DMA((pieces,)),
        ],
        compiler_params=pltpu.CompilerParams(
            collective_id=0, has_side_effects=True, vmem_limit_bytes=63 * 1024 * 1024
        ),
    )(slc, pairs.T, inverse)


def solution(mesh):
    n = mesh.shape["date"]
    in_specs = (P("date", None, "grp", None), P(), P())
    out_specs = P(None, ("grp", "date"), None)
    return jax.shard_map(
        functools.partial(per_device, n),
        mesh=mesh,
        in_specs=in_specs,
        out_specs=out_specs,
        check_vma=False,
    )
```

```python
import functools

import jax
import jax.numpy as jnp
from jax import lax
from jax.experimental import pallas as pl
from jax.experimental.pallas import tpu as pltpu
from jax.sharding import PartitionSpec as P

LOOK_R = 4
LOOK_C = 16
LANES = 128
BLOCK = 16
PIECES = 1


def split(x):
    high = x.astype(jnp.bfloat16)
    low = (x - high.astype(jnp.float32)).astype(jnp.bfloat16)
    return high, low


def kernel(
    n,
    pieces,
    slc_hbm,
    pairs_hbm,
    inverse_hbm,
    out_ref,
    tile,
    pairs,
    pairs_v,
    inverse,
    stage,
    send,
    recv,
    held,
    rowsum,
    window,
    hot,
    in_sem,
    small_sem,
    send_sem,
    recv_sem,
):
    me = lax.axis_index("date")
    half = n // 2
    rows, cols = tile.shape[1], tile.shape[2]
    chunks = cols // LANES // pieces
    pitch = chunks + 1
    span = LOOK_R * chunks
    blocks = rows // BLOCK
    near = blocks // 2
    per = BLOCK // LOOK_R
    npair = pairs.shape[1]
    total = npair + n
    group = rowsum.shape[0] // total - 1
    base = (me // half) * half
    other = half - base
    block_base = (me // half) * near

    phase = (me // per) % 2

    def block_at(k):
        turn = k // 2
        far = jnp.where(me < half, blocks - 1 - turn, turn)
        own = block_base + (me // per + 1 + turn) % near
        return jnp.where((k + phase) % 2 == 0, far, own)

    def load(k):
        at = pl.ds(pl.multiple_of(block_at(k) * BLOCK, BLOCK), BLOCK)
        return pltpu.make_async_copy(
            slc_hbm.at[0, :, at, :], tile.at[:, at, :], in_sem.at[k]
        )

    smalls = [
        pltpu.make_async_copy(pairs_hbm, pairs, small_sem.at[0]),
        pltpu.make_async_copy(pairs_hbm, pairs_v, small_sem.at[1]),
        pltpu.make_async_copy(inverse_hbm, inverse, small_sem.at[2]),
    ]
    barrier = pltpu.get_barrier_semaphore()

    for k in [*range(half, n), *range(1, half)]:
        pl.semaphore_signal(
            barrier,
            inc=1,
            device_id={"date": (me + k) % n},
            device_id_type=pl.DeviceIdType.MESH,
        )
    for k in range(blocks):
        load(k).start()
    for copy in smalls:
        copy.start()

    def regroup(k):
        block = block_at(k)
        at = pl.ds(pl.multiple_of(block * BLOCK, BLOCK), BLOCK)
        for q in range(pieces):
            for part in range(2):
                for c in range(chunks):
                    column = (q * chunks + c) * LANES
                    piece = tile[part, at, column : column + LANES].astype(jnp.float32)
                    stage[q, part, pl.ds(c, BLOCK, stride=pitch), :] = piece
            for row in range(BLOCK):
                for part in range(2):
                    at = row % LOOK_R * chunks
                    piece = stage[q, part, row * pitch : row * pitch + chunks, :]
                    send[q, block * per + row // LOOK_R, part, at : at + chunks] = (
                        piece.astype(jnp.bfloat16)
                    )

    def remote(q, to, came):
        return pltpu.make_async_remote_copy(
            src_ref=send.at[q, to],
            dst_ref=recv.at[q, came],
            send_sem=send_sem.at[q],
            recv_sem=recv_sem.at[q, (to // half + me // half) % 2],
            device_id={"date": to},
            device_id_type=pl.DeviceIdType.MESH,
        )

    def every(q, side, count):
        return pltpu.make_async_remote_copy(
            src_ref=send.at[q, pl.ds(0, count)],
            dst_ref=recv.at[q, pl.ds(0, count)],
            send_sem=send_sem.at[q],
            recv_sem=recv_sem.at[q, side],
            device_id={"date": (me + 1) % n},
            device_id_type=pl.DeviceIdType.MESH,
        )

    def post(q, k):
        block = block_at(k)
        for j in range(per):
            to = block * per + (me + j) % per

            @pl.when(to != me)
            def _():
                remote(q, to, me).start()

    def fill(k, _):
        load(k).wait()
        regroup(k)

        @pl.when(k == 0)
        def _():
            pl.semaphore_wait(barrier, n - 1)

        post(0, k)
        return 0

    lax.fori_loop(0, blocks, fill, 0)

    def more(k, _):
        post(1 + k // blocks, k % blocks)
        return 0

    lax.fori_loop(0, (pieces - 1) * blocks, more, 0)

    for copy in smalls:
        copy.wait()

    def tile_of_window(c, _):
        shape = (LANES, window.shape[1])
        col = c * (LANES // LOOK_C) + lax.broadcasted_iota(jnp.int32, shape, 0) // LOOK_C
        win = lax.broadcasted_iota(jnp.int32, shape, 1)
        at = pl.ds(pl.multiple_of(c * LANES, LANES), LANES)
        window[at, :] = jnp.where(col == win, 1.0, 0.0).astype(jnp.bfloat16)
        return 0

    lax.fori_loop(0, cols // LANES, tile_of_window, 0)
    date = lax.broadcasted_iota(jnp.int32, (n, npair), 0)
    for which in range(2):
        flag = jnp.where(pairs_v[which : which + 1, :] == date, 1.0, 0.0)
        hot[which * npair : (which + 1) * npair, :] = flag.T.astype(jnp.bfloat16)
    for q in range(pieces):
        recv[q, me] = send[q, me]

    def keep(row, x):
        rowsum[pl.ds(row * (group + 1), group), :] = x.reshape(-1, group, LANES).sum(axis=0)

    def piece_of(q, looked):
        def power(t):
            x = recv[q, t].astype(jnp.float32)
            held[t] = x
            keep(npair + t, x[0] * x[0] + x[1] * x[1])

        def powers_from(first):
            def one(k, _):
                power(first + k)
                return 0

            lax.fori_loop(0, half, one, 0, unroll=4)

        def pair(p, _):
            a = held[pairs[0, p]]
            b = held[pairs[1, p]]
            keep(p, a[1] * b[0] - a[0] * b[1])
            return 0

        every(q, 0, half - 1).wait_recv()
        powers_from(base)
        every(q, 1, half).wait_recv()
        powers_from(other)
        lax.fori_loop(0, npair, pair, 0, unroll=8)

        columns = []
        for c in range(chunks):
            x = rowsum[pl.ds(c, total, stride=group + 1), :]
            for again in range(c + chunks, group, chunks):
                x += rowsum[pl.ds(again, total, stride=group + 1), :]
            columns.append(x)
        high, low = split(jnp.concatenate(columns, axis=1))
        depth = chunks * LANES
        sums = jnp.dot(
            jnp.concatenate([high, low], axis=0),
            window[pl.ds(pl.multiple_of(q * depth, depth), depth), :],
            preferred_element_type=jnp.float32,
        )
        return looked + sums[:total] + sums[total:]

    looked = jnp.zeros((total, window.shape[1]), jnp.float32)
    looked = lax.fori_loop(0, pieces, piece_of, looked)

    def exact(left, x):
        width = x.shape[1]
        both = jnp.concatenate(split(x), axis=1)
        y = jnp.dot(left, both, preferred_element_type=jnp.float32)
        return y[:, :width] + y[:, width:]

    powers = exact(hot[...], looked[npair:])
    proxy = looked[:npair] * lax.rsqrt(powers[:npair] * powers[npair:] + 1e-06)
    out_ref[...] = exact(inverse[...], proxy).reshape(out_ref.shape)

    for q in range(pieces):
        every(q, 0, n - 1).wait_send()


def per_device(n, slc, pairs, inverse):
    _, _, rows, cols = slc.shape
    steps, npair = inverse.shape
    pieces = PIECES
    chunks = cols // LANES // pieces
    span = LOOK_R * chunks
    group = max(chunks, 8)
    windows = cols // LOOK_C
    return pl.pallas_call(
        functools.partial(kernel, n, pieces),
        out_shape=pltpu.VMEM((steps, 1, windows), jnp.float32),
        in_specs=[pl.BlockSpec(memory_space=pltpu.HBM)] * 3,
        out_specs=pl.BlockSpec(memory_space=pltpu.VMEM),
        scratch_shapes=[
            pltpu.VMEM((2, rows, cols), jnp.bfloat16),
            pltpu.SMEM((2, npair), jnp.int32),
            pltpu.VMEM((2, npair), jnp.int32),
            pltpu.VMEM((steps, npair), jnp.bfloat16),
            pltpu.VMEM((pieces, 2, BLOCK * (chunks + 1), LANES), jnp.float32),
            pltpu.VMEM((pieces, n, 2, span, LANES), jnp.bfloat16),
            pltpu.VMEM((pieces, n, 2, span, LANES), jnp.bfloat16),
            pltpu.VMEM((n, 2, span, LANES), jnp.float32),
            pltpu.VMEM(((npair + n) * (group + 1), LANES), jnp.float32),
            pltpu.VMEM((cols, windows), jnp.bfloat16),
            pltpu.VMEM((2 * npair, n), jnp.bfloat16),
            pltpu.SemaphoreType.DMA((rows // BLOCK,)),
            pltpu.SemaphoreType.DMA((3,)),
            pltpu.SemaphoreType.DMA((pieces,)),
            pltpu.SemaphoreType.DMA((pieces, 2)),
        ],
        compiler_params=pltpu.CompilerParams(
            collective_id=0, has_side_effects=True, vmem_limit_bytes=63 * 1024 * 1024
        ),
    )(slc, pairs.T, inverse)


def solution(mesh):
    n = mesh.shape["date"]
    in_specs = (P("date", None, "grp", None), P(), P())
    out_specs = P(None, ("grp", "date"), None)
    return jax.shard_map(
        functools.partial(per_device, n),
        mesh=mesh,
        in_specs=in_specs,
        out_specs=out_specs,
        check_vma=False,
    )
```

```python
import functools

import jax
import jax.numpy as jnp
from jax import lax
from jax.experimental import pallas as pl
from jax.experimental.pallas import tpu as pltpu
from jax.sharding import PartitionSpec as P

LOOK_R = 4
LOOK_C = 16
LANES = 128
BLOCK = 16
PIECES = 1


def split(x):
    high = x.astype(jnp.bfloat16)
    low = (x - high.astype(jnp.float32)).astype(jnp.bfloat16)
    return high, low


def kernel(
    n,
    pieces,
    slc_hbm,
    pairs_hbm,
    inverse_hbm,
    out_ref,
    tile,
    pairs,
    pairs_v,
    inverse,
    stage,
    send,
    recv,
    held,
    rowsum,
    window,
    hot,
    in_sem,
    small_sem,
    send_sem,
    recv_sem,
):
    me = lax.axis_index("date")
    half = n // 2
    rows, cols = tile.shape[1], tile.shape[2]
    chunks = cols // LANES // pieces
    pitch = chunks + 1
    span = LOOK_R * chunks
    blocks = rows // BLOCK
    near = blocks // 2
    per = BLOCK // LOOK_R
    npair = pairs.shape[1]
    total = npair + n
    group = rowsum.shape[0] // total - 1
    base = (me // half) * half
    other = half - base
    block_base = (me // half) * near


    def block_at(k):
        turn = k // 2
        far = jnp.where(me < half, blocks - 1 - turn, turn)
        own = block_base + (me // per + 1 + turn) % near
        return jnp.where(k % 2 == 0, far, own)

    def load(k):
        at = pl.ds(pl.multiple_of(block_at(k) * BLOCK, BLOCK), BLOCK)
        return pltpu.make_async_copy(
            slc_hbm.at[0, :, at, :], tile.at[:, at, :], in_sem.at[k]
        )

    smalls = [
        pltpu.make_async_copy(pairs_hbm, pairs, small_sem.at[0]),
        pltpu.make_async_copy(pairs_hbm, pairs_v, small_sem.at[1]),
        pltpu.make_async_copy(inverse_hbm, inverse, small_sem.at[2]),
    ]
    barrier = pltpu.get_barrier_semaphore()

    for k in [*range(half, n), *range(1, half)]:
        pl.semaphore_signal(
            barrier,
            inc=1,
            device_id={"date": (me + k) % n},
            device_id_type=pl.DeviceIdType.MESH,
        )
    for k in range(blocks):
        load(k).start()
    for copy in smalls:
        copy.start()

    def regroup(k):
        block = block_at(k)
        at = pl.ds(pl.multiple_of(block * BLOCK, BLOCK), BLOCK)
        for q in range(pieces):
            for part in range(2):
                for c in range(chunks):
                    column = (q * chunks + c) * LANES
                    piece = tile[part, at, column : column + LANES].astype(jnp.float32)
                    stage[q, part, pl.ds(c, BLOCK, stride=pitch), :] = piece
            for row in range(BLOCK):
                for part in range(2):
                    at = row % LOOK_R * chunks
                    piece = stage[q, part, row * pitch : row * pitch + chunks, :]
                    send[q, block * per + row // LOOK_R, part, at : at + chunks] = (
                        piece.astype(jnp.bfloat16)
                    )

    def remote(q, to, came):
        return pltpu.make_async_remote_copy(
            src_ref=send.at[q, to],
            dst_ref=recv.at[q, came],
            send_sem=send_sem.at[q],
            recv_sem=recv_sem.at[q, (to // half + me // half) % 2],
            device_id={"date": to},
            device_id_type=pl.DeviceIdType.MESH,
        )

    def every(q, side, count):
        return pltpu.make_async_remote_copy(
            src_ref=send.at[q, pl.ds(0, count)],
            dst_ref=recv.at[q, pl.ds(0, count)],
            send_sem=send_sem.at[q],
            recv_sem=recv_sem.at[q, side],
            device_id={"date": (me + 1) % n},
            device_id_type=pl.DeviceIdType.MESH,
        )

    def post(q, k):
        block = block_at(k)
        for j in range(per):
            to = block * per + (me + j) % per

            @pl.when(to != me)
            def _():
                remote(q, to, me).start()

    def fill(k, _):
        load(k).wait()
        regroup(k)

        @pl.when(k == 0)
        def _():
            pl.semaphore_wait(barrier, n - 1)

        post(0, k)
        return 0

    lax.fori_loop(0, blocks, fill, 0)

    def more(k, _):
        post(1 + k // blocks, k % blocks)
        return 0

    lax.fori_loop(0, (pieces - 1) * blocks, more, 0)

    for copy in smalls:
        copy.wait()

    def tile_of_window(c, _):
        shape = (LANES, window.shape[1])
        col = c * (LANES // LOOK_C) + lax.broadcasted_iota(jnp.int32, shape, 0) // LOOK_C
        win = lax.broadcasted_iota(jnp.int32, shape, 1)
        at = pl.ds(pl.multiple_of(c * LANES, LANES), LANES)
        window[at, :] = jnp.where(col == win, 1.0, 0.0).astype(jnp.bfloat16)
        return 0

    lax.fori_loop(0, cols // LANES, tile_of_window, 0)
    date = lax.broadcasted_iota(jnp.int32, (n, npair), 0)
    for which in range(2):
        flag = jnp.where(pairs_v[which : which + 1, :] == date, 1.0, 0.0)
        hot[which * npair : (which + 1) * npair, :] = flag.T.astype(jnp.bfloat16)
    for q in range(pieces):
        recv[q, me] = send[q, me]

    def keep(row, x):
        rowsum[pl.ds(row * (group + 1), group), :] = x.reshape(-1, group, LANES).sum(axis=0)

    def piece_of(q, looked):
        def power(t):
            x = recv[q, t].astype(jnp.float32)
            held[t] = x
            keep(npair + t, x[0] * x[0] + x[1] * x[1])

        def powers_from(first):
            def one(k, _):
                power(first + k)
                return 0

            lax.fori_loop(0, half, one, 0, unroll=4)

        def pair(p, _):
            a = held[pairs[0, p]]
            b = held[pairs[1, p]]
            keep(p, a[1] * b[0] - a[0] * b[1])
            return 0

        every(q, 0, half - 1).wait_recv()
        powers_from(base)
        every(q, 1, half).wait_recv()
        powers_from(other)
        lax.fori_loop(0, npair, pair, 0, unroll=8)

        columns = []
        for c in range(chunks):
            x = rowsum[pl.ds(c, total, stride=group + 1), :]
            for again in range(c + chunks, group, chunks):
                x += rowsum[pl.ds(again, total, stride=group + 1), :]
            columns.append(x)
        high, low = split(jnp.concatenate(columns, axis=1))
        depth = chunks * LANES
        sums = jnp.dot(
            jnp.concatenate([high, low], axis=0),
            window[pl.ds(pl.multiple_of(q * depth, depth), depth), :],
            preferred_element_type=jnp.float32,
        )
        return looked + sums[:total] + sums[total:]

    looked = jnp.zeros((total, window.shape[1]), jnp.float32)
    looked = lax.fori_loop(0, pieces, piece_of, looked)

    def exact(left, x):
        width = x.shape[1]
        both = jnp.concatenate(split(x), axis=1)
        y = jnp.dot(left, both, preferred_element_type=jnp.float32)
        return y[:, :width] + y[:, width:]

    powers = exact(hot[...], looked[npair:])
    proxy = looked[:npair] * lax.rsqrt(powers[:npair] * powers[npair:] + 1e-06)
    out_ref[...] = exact(inverse[...], proxy).reshape(out_ref.shape)

    for q in range(pieces):
        every(q, 0, n - 1).wait_send()


def per_device(n, slc, pairs, inverse):
    _, _, rows, cols = slc.shape
    steps, npair = inverse.shape
    pieces = PIECES
    chunks = cols // LANES // pieces
    span = LOOK_R * chunks
    group = max(chunks, 8)
    windows = cols // LOOK_C
    return pl.pallas_call(
        functools.partial(kernel, n, pieces),
        out_shape=pltpu.VMEM((steps, 1, windows), jnp.float32),
        in_specs=[pl.BlockSpec(memory_space=pltpu.HBM)] * 3,
        out_specs=pl.BlockSpec(memory_space=pltpu.VMEM),
        scratch_shapes=[
            pltpu.VMEM((2, rows, cols), jnp.bfloat16),
            pltpu.SMEM((2, npair), jnp.int32),
            pltpu.VMEM((2, npair), jnp.int32),
            pltpu.VMEM((steps, npair), jnp.bfloat16),
            pltpu.VMEM((pieces, 2, BLOCK * (chunks + 1), LANES), jnp.float32),
            pltpu.VMEM((pieces, n, 2, span, LANES), jnp.bfloat16),
            pltpu.VMEM((pieces, n, 2, span, LANES), jnp.bfloat16),
            pltpu.VMEM((n, 2, span, LANES), jnp.float32),
            pltpu.VMEM(((npair + n) * (group + 1), LANES), jnp.float32),
            pltpu.VMEM((cols, windows), jnp.bfloat16),
            pltpu.VMEM((2 * npair, n), jnp.bfloat16),
            pltpu.SemaphoreType.DMA((rows // BLOCK,)),
            pltpu.SemaphoreType.DMA((3,)),
            pltpu.SemaphoreType.DMA((pieces,)),
            pltpu.SemaphoreType.DMA((pieces, 2)),
        ],
        compiler_params=pltpu.CompilerParams(
            collective_id=0, has_side_effects=True, vmem_limit_bytes=63 * 1024 * 1024
        ),
    )(slc, pairs.T, inverse)


def solution(mesh):
    n = mesh.shape["date"]
    in_specs = (P("date", None, "grp", None), P(), P())
    out_specs = P(None, ("grp", "date"), None)
    return jax.shard_map(
        functools.partial(per_device, n),
        mesh=mesh,
        in_specs=in_specs,
        out_specs=out_specs,
        check_vma=False,
    )
```

```python
import functools

import jax
import jax.numpy as jnp
from jax import lax
from jax.experimental import pallas as pl
from jax.experimental.pallas import tpu as pltpu
from jax.sharding import PartitionSpec as P

LOOK_R = 4
LOOK_C = 16
LANES = 128
BLOCK = 16
PIECES = 1


def split(x):
    high = x.astype(jnp.bfloat16)
    low = (x - high.astype(jnp.float32)).astype(jnp.bfloat16)
    return high, low


def kernel(
    n,
    pieces,
    slc_hbm,
    pairs_hbm,
    inverse_hbm,
    out_ref,
    tile,
    pairs,
    pairs_v,
    inverse,
    stage,
    send,
    recv,
    held,
    rowsum,
    window,
    hot,
    in_sem,
    small_sem,
    send_sem,
    recv_sem,
):
    me = lax.axis_index("date")
    half = n // 2
    rows, cols = tile.shape[1], tile.shape[2]
    chunks = cols // LANES // pieces
    pitch = chunks + 1
    span = LOOK_R * chunks
    blocks = rows // BLOCK
    near = blocks // 2
    per = BLOCK // LOOK_R
    npair = pairs.shape[1]
    total = npair + n
    group = rowsum.shape[0] // total - 1
    base = (me // half) * half
    other = half - base
    block_base = (me // half) * near


    def block_at(k):
        turn = k // 2
        far = jnp.where(me < half, near + turn, turn)
        own = block_base + (me // per + 1 + turn) % near
        return jnp.where(k % 2 == 0, far, own)

    def load(k):
        at = pl.ds(pl.multiple_of(block_at(k) * BLOCK, BLOCK), BLOCK)
        return pltpu.make_async_copy(
            slc_hbm.at[0, :, at, :], tile.at[:, at, :], in_sem.at[k]
        )

    smalls = [
        pltpu.make_async_copy(pairs_hbm, pairs, small_sem.at[0]),
        pltpu.make_async_copy(pairs_hbm, pairs_v, small_sem.at[1]),
        pltpu.make_async_copy(inverse_hbm, inverse, small_sem.at[2]),
    ]
    barrier = pltpu.get_barrier_semaphore()

    for k in [*range(half, n), *range(1, half)]:
        pl.semaphore_signal(
            barrier,
            inc=1,
            device_id={"date": (me + k) % n},
            device_id_type=pl.DeviceIdType.MESH,
        )
    for k in range(blocks):
        load(k).start()
    for copy in smalls:
        copy.start()

    def regroup(k):
        block = block_at(k)
        at = pl.ds(pl.multiple_of(block * BLOCK, BLOCK), BLOCK)
        for q in range(pieces):
            for part in range(2):
                for c in range(chunks):
                    column = (q * chunks + c) * LANES
                    piece = tile[part, at, column : column + LANES].astype(jnp.float32)
                    stage[q, part, pl.ds(c, BLOCK, stride=pitch), :] = piece
            for row in range(BLOCK):
                for part in range(2):
                    at = row % LOOK_R * chunks
                    piece = stage[q, part, row * pitch : row * pitch + chunks, :]
                    send[q, block * per + row // LOOK_R, part, at : at + chunks] = (
                        piece.astype(jnp.bfloat16)
                    )

    def remote(q, to, came):
        return pltpu.make_async_remote_copy(
            src_ref=send.at[q, to],
            dst_ref=recv.at[q, came],
            send_sem=send_sem.at[q],
            recv_sem=recv_sem.at[q, (to // half + me // half) % 2],
            device_id={"date": to},
            device_id_type=pl.DeviceIdType.MESH,
        )

    def every(q, side, count):
        return pltpu.make_async_remote_copy(
            src_ref=send.at[q, pl.ds(0, count)],
            dst_ref=recv.at[q, pl.ds(0, count)],
            send_sem=send_sem.at[q],
            recv_sem=recv_sem.at[q, side],
            device_id={"date": (me + 1) % n},
            device_id_type=pl.DeviceIdType.MESH,
        )

    def post(q, k):
        block = block_at(k)
        for j in range(per):
            to = block * per + (me + j) % per

            @pl.when(to != me)
            def _():
                remote(q, to, me).start()

    def fill(k, _):
        load(k).wait()
        regroup(k)

        @pl.when(k == 0)
        def _():
            pl.semaphore_wait(barrier, n - 1)

        post(0, k)
        return 0

    lax.fori_loop(0, blocks, fill, 0)

    def more(k, _):
        post(1 + k // blocks, k % blocks)
        return 0

    lax.fori_loop(0, (pieces - 1) * blocks, more, 0)

    for copy in smalls:
        copy.wait()

    def tile_of_window(c, _):
        shape = (LANES, window.shape[1])
        col = c * (LANES // LOOK_C) + lax.broadcasted_iota(jnp.int32, shape, 0) // LOOK_C
        win = lax.broadcasted_iota(jnp.int32, shape, 1)
        at = pl.ds(pl.multiple_of(c * LANES, LANES), LANES)
        window[at, :] = jnp.where(col == win, 1.0, 0.0).astype(jnp.bfloat16)
        return 0

    lax.fori_loop(0, cols // LANES, tile_of_window, 0)
    date = lax.broadcasted_iota(jnp.int32, (n, npair), 0)
    for which in range(2):
        flag = jnp.where(pairs_v[which : which + 1, :] == date, 1.0, 0.0)
        hot[which * npair : (which + 1) * npair, :] = flag.T.astype(jnp.bfloat16)
    for q in range(pieces):
        recv[q, me] = send[q, me]

    def keep(row, x):
        rowsum[pl.ds(row * (group + 1), group), :] = x.reshape(-1, group, LANES).sum(axis=0)

    def piece_of(q, looked):
        def power(t):
            x = recv[q, t].astype(jnp.float32)
            held[t] = x
            keep(npair + t, x[0] * x[0] + x[1] * x[1])

        def powers_from(first):
            def one(k, _):
                power(first + k)
                return 0

            lax.fori_loop(0, half, one, 0, unroll=4)

        def pair(p, _):
            a = held[pairs[0, p]]
            b = held[pairs[1, p]]
            keep(p, a[1] * b[0] - a[0] * b[1])
            return 0

        every(q, 0, half - 1).wait_recv()
        powers_from(base)
        every(q, 1, half).wait_recv()
        powers_from(other)
        lax.fori_loop(0, npair, pair, 0, unroll=16)

        columns = []
        for c in range(chunks):
            x = rowsum[pl.ds(c, total, stride=group + 1), :]
            for again in range(c + chunks, group, chunks):
                x += rowsum[pl.ds(again, total, stride=group + 1), :]
            columns.append(x)
        high, low = split(jnp.concatenate(columns, axis=1))
        depth = chunks * LANES
        sums = jnp.dot(
            jnp.concatenate([high, low], axis=0),
            window[pl.ds(pl.multiple_of(q * depth, depth), depth), :],
            preferred_element_type=jnp.float32,
        )
        return looked + sums[:total] + sums[total:]

    looked = jnp.zeros((total, window.shape[1]), jnp.float32)
    looked = lax.fori_loop(0, pieces, piece_of, looked)

    def exact(left, x):
        width = x.shape[1]
        both = jnp.concatenate(split(x), axis=1)
        y = jnp.dot(left, both, preferred_element_type=jnp.float32)
        return y[:, :width] + y[:, width:]

    powers = exact(hot[...], looked[npair:])
    proxy = looked[:npair] * lax.rsqrt(powers[:npair] * powers[npair:] + 1e-06)
    out_ref[...] = exact(inverse[...], proxy).reshape(out_ref.shape)

    for q in range(pieces):
        every(q, 0, n - 1).wait_send()


def per_device(n, slc, pairs, inverse):
    _, _, rows, cols = slc.shape
    steps, npair = inverse.shape
    pieces = PIECES
    chunks = cols // LANES // pieces
    span = LOOK_R * chunks
    group = max(chunks, 8)
    windows = cols // LOOK_C
    return pl.pallas_call(
        functools.partial(kernel, n, pieces),
        out_shape=pltpu.VMEM((steps, 1, windows), jnp.float32),
        in_specs=[pl.BlockSpec(memory_space=pltpu.HBM)] * 3,
        out_specs=pl.BlockSpec(memory_space=pltpu.VMEM),
        scratch_shapes=[
            pltpu.VMEM((2, rows, cols), jnp.bfloat16),
            pltpu.SMEM((2, npair), jnp.int32),
            pltpu.VMEM((2, npair), jnp.int32),
            pltpu.VMEM((steps, npair), jnp.bfloat16),
            pltpu.VMEM((pieces, 2, BLOCK * (chunks + 1), LANES), jnp.float32),
            pltpu.VMEM((pieces, n, 2, span, LANES), jnp.bfloat16),
            pltpu.VMEM((pieces, n, 2, span, LANES), jnp.bfloat16),
            pltpu.VMEM((n, 2, span, LANES), jnp.float32),
            pltpu.VMEM(((npair + n) * (group + 1), LANES), jnp.float32),
            pltpu.VMEM((cols, windows), jnp.bfloat16),
            pltpu.VMEM((2 * npair, n), jnp.bfloat16),
            pltpu.SemaphoreType.DMA((rows // BLOCK,)),
            pltpu.SemaphoreType.DMA((3,)),
            pltpu.SemaphoreType.DMA((pieces,)),
            pltpu.SemaphoreType.DMA((pieces, 2)),
        ],
        compiler_params=pltpu.CompilerParams(
            collective_id=0, has_side_effects=True, vmem_limit_bytes=63 * 1024 * 1024
        ),
    )(slc, pairs.T, inverse)


def solution(mesh):
    n = mesh.shape["date"]
    in_specs = (P("date", None, "grp", None), P(), P())
    out_specs = P(None, ("grp", "date"), None)
    return jax.shard_map(
        functools.partial(per_device, n),
        mesh=mesh,
        in_specs=in_specs,
        out_specs=out_specs,
        check_vma=False,
    )
```
